768 devices in a mesh: rows: 24 (over z_lo, x), task: 32 (over z_hi, y, core).
Axes of the slice: x: 4, y: 8, z: 12 (z_hi: 2, z_lo: 6; z = z_hi * 6 + z_lo), core: 2. Of those that a mesh axis runs over, the one named last changes fastest.
Arguments:
- hamiltonian_tiles: bfloat16 [24576, 4096], P(('rows', 'task')), may hold values from -0.1875 to 0.1875
- tile_target: int32 [24576], P(('rows', 'task')), may hold values from 0 to 767, as said below
- column_block: int32 [24576], P(('rows', 'task')), may hold values from 0 to 1535, as said below
- row_count: int32 [1536], P(('rows', 'task')), may hold values from 1 to 16
- vectors: bfloat16 [192, 98304], P('task', 'rows'), may hold values from -6 to 6
- expansion_coef: float32 [5], replicated, may hold values from -3 to 3
Outputs:
- fermi_vectors: bfloat16 [192, 98304], P('task', 'rows')
The draws below stay inside these ranges and needn't reach their ends.
Inputs may be any that keep to these rules, and one draw needn't show every extreme that they name: `tile_target`: for each task index, the values on the 24 devices of that task index together are each of 0 to 767 once; a device sends none or exactly 2 of its blocks to any device of the rows axis. `column_block`: slot 0 of block row g names column block g; the other slots name column blocks within 8 of g, distinct except near the matrix's ends, where the numbers are cut to 0 and 1535 and may repeat.
All inputs are finite; a program needn't handle non-finite values.
Results may differ from the reference program's by a relative error of at most 0.013.
Values may be sent and summed in bfloat16 or wider, within the bound.
A program may use at most 64 MiB of HBM per device.

```python
import jax
import jax.numpy as jnp
from jax import lax

TILE = 64
SLOTS_ROW = 16
BLOCK_ROWS = 2
REACH = 8
ITERS = 4
VECTORS = 192
NBLOCKS = 1536
SLOTS_DEV = 32
N_ROWS = 24
N_TASK = 32
DEVICES = 768


def draw_tile_target(key, part):
    key = jax.random.fold_in(key, 13)
    slots_dev = BLOCK_ROWS * SLOTS_ROW
    capacity = max(2, slots_dev // min(N_ROWS, 16))
    offsets_n = slots_dev // capacity
    key_base, key_label, key_order = jax.random.split(key, 3)
    base = jax.vmap(lambda subkey: jax.random.permutation(subkey, N_ROWS)[:offsets_n])(jax.random.split(key_base, N_TASK))
    shifts = jnp.repeat(base, capacity, axis=1)
    labels = jax.vmap(lambda subkey: jax.random.permutation(subkey, slots_dev))(jax.random.split(key_label, N_ROWS * N_TASK))
    labels = labels.reshape(N_ROWS, N_TASK, slots_dev)
    source = jnp.arange(N_ROWS, dtype=jnp.int32)[:, None, None]
    group = jnp.arange(N_TASK, dtype=jnp.int32)[None, :, None]
    within = jnp.arange(slots_dev, dtype=jnp.int32)[None, None, :]
    owner = (source - shifts[None, :, :].astype(jnp.int32)) % N_ROWS
    values = owner * slots_dev + labels[owner, group, within].astype(jnp.int32)
    shuffle = jax.vmap(lambda subkey: jax.random.permutation(subkey, slots_dev))(jax.random.split(key_order, N_ROWS * N_TASK))
    shuffle = shuffle.reshape(N_ROWS, N_TASK, slots_dev).astype(jnp.int32)
    return jnp.take_along_axis(values, shuffle, axis=2).reshape(-1).astype(jnp.int32)


def draw_column_block(key, part):
    key = jax.random.fold_in(key, 11)
    nblocks = BLOCK_ROWS * N_TASK * N_ROWS

    def one_row(subkey):
        picks = jax.random.permutation(subkey, 2 * REACH)[:SLOTS_ROW - 1].astype(jnp.int32)
        picks = jnp.where(picks < REACH, picks - REACH, picks - REACH + 1)
        return jnp.concatenate([jnp.zeros((1,), jnp.int32), picks])
    offsets = jax.vmap(one_row)(jax.random.split(key, nblocks))
    anchor = jnp.arange(nblocks, dtype=jnp.int32)[:, None]
    return jnp.clip(anchor + offsets, 0, nblocks - 1).reshape(-1).astype(jnp.int32)


def draw_row_count(key, part):
    key = jax.random.fold_in(key, 12)
    nblocks = BLOCK_ROWS * N_TASK * N_ROWS
    key_heavy, key_count = jax.random.split(key)
    heavy = jax.random.randint(key_heavy, (N_ROWS * N_TASK,), 0, 4) == 0
    ceiling = jnp.where(heavy, SLOTS_ROW, SLOTS_ROW // 2).astype(jnp.int32)
    ceiling = jnp.repeat(ceiling, BLOCK_ROWS)
    counts = jax.random.randint(key_count, (nblocks,), 1, ceiling + 1).astype(jnp.int32)
    return counts.at[0].set(SLOTS_ROW)


def shard_levels(own_key, shape, shards, least, largest):
    gain, own = 1.0, jax.random.fold_in(own_key, 6)
    for axis_at, parts in shards:
        heights = jnp.exp(jax.random.uniform(jax.random.fold_in(own, axis_at), (parts,), jnp.float32, least / len(shards), largest / len(shards)))
        gain = gain * jnp.repeat(heights, shape[axis_at] // parts).reshape([-1 if axis == axis_at else 1 for axis in range(len(shape))])
    return gain


def centred(own_key, shape, deviation, bound, cuts=(), held_as=jnp.bfloat16):
    factor_of = shard_levels(own_key, shape, cuts, -0.22, 0.18) if cuts else 1.0
    drawn = jax.random.normal(own_key, shape, jnp.float32) * deviation * factor_of
    return jnp.minimum(jnp.maximum(drawn, -bound), bound).astype(held_as)


def setup_inputs(seed: int = 0) -> dict:
    splits = jax.random.split(jax.random.key(seed), 7)
    hamiltonian_tiles = centred(splits[0], (DEVICES * SLOTS_DEV, TILE * TILE), (SLOTS_ROW * TILE) ** -0.5, 0.1875, ((0, 768),))
    tile_target = draw_tile_target(jax.random.fold_in(splits[6], 71), 0)
    column_block = draw_column_block(jax.random.fold_in(splits[6], 71), 0)
    row_count = draw_row_count(jax.random.fold_in(splits[6], 71), 0)
    vectors = centred(splits[4], (VECTORS, NBLOCKS * TILE), 1.0, 6.0, ((0, 32), (1, 24)))
    expansion_coef = centred(splits[5], (ITERS + 1,), 1.0, 3.0, (), jnp.float32)
    return {"hamiltonian_tiles": hamiltonian_tiles, "tile_target": tile_target, "column_block": column_block, "row_count": row_count, "vectors": vectors, "expansion_coef": expansion_coef}


def reference(hamiltonian_tiles, tile_target, column_block, row_count, vectors, expansion_coef):
    slots_dev = BLOCK_ROWS * SLOTS_ROW
    nblocks = BLOCK_ROWS * N_TASK * N_ROWS
    per_panel = BLOCK_ROWS * N_TASK
    sources = hamiltonian_tiles.reshape(N_ROWS, N_TASK, slots_dev, TILE * TILE)
    sources = sources.transpose(1, 0, 2, 3).reshape(N_TASK, N_ROWS * slots_dev, TILE * TILE)
    targets = tile_target.reshape(N_ROWS, N_TASK, slots_dev).transpose(1, 0, 2).reshape(N_TASK, N_ROWS * slots_dev)

    def put_blocks(tiles, where):
        return jnp.zeros_like(tiles).at[where].set(tiles)

    placed = jax.vmap(put_blocks)(sources, targets)
    placed = placed.reshape(N_TASK, N_ROWS, slots_dev, TILE * TILE).transpose(1, 0, 2, 3)
    placed = placed.reshape(nblocks, SLOTS_ROW, TILE, TILE)
    live = (jnp.arange(SLOTS_ROW, dtype=jnp.int32)[None, :] < row_count[:, None]).astype(jnp.bfloat16)
    blocks = placed * live[:, :, None, None]
    panel_blocks = blocks.reshape(N_ROWS, per_panel, SLOTS_ROW, TILE, TILE)
    panel_cols = column_block.reshape(N_ROWS, per_panel, SLOTS_ROW)

    def apply_matrix(current):
        pieces = current.reshape(VECTORS, nblocks, TILE)

        def one_panel(operands):
            tiles, where = operands
            picked = pieces[:, where, :].astype(jnp.float32)
            return jnp.einsum('nikb,ikab->nia', picked, tiles.astype(jnp.float32))

        result = lax.map(one_panel, (panel_blocks, panel_cols))
        return result.transpose(1, 0, 2, 3).reshape(VECTORS, nblocks * TILE)

    previous = vectors
    total = expansion_coef[0] * vectors.astype(jnp.float32)
    current = apply_matrix(vectors).astype(jnp.bfloat16)
    total = total + expansion_coef[1] * current.astype(jnp.float32)
    for order in range(2, ITERS + 1):
        product = apply_matrix(current)
        following = (2.0 * product - previous.astype(jnp.float32)).astype(jnp.bfloat16)
        total = total + expansion_coef[order] * following.astype(jnp.float32)
        previous, current = current, following
    return total.astype(jnp.bfloat16)
```

```python
import jax
import jax.numpy as jnp
from jax import lax
from jax.experimental import pallas as pl
from jax.experimental.pallas import tpu as pltpu
from jax.sharding import PartitionSpec as P

TILE = 64
SLOTS_ROW = 16
REACH = 8
ITERS = 4
MESH = pl.DeviceIdType.MESH
F32 = jnp.float32
BF16 = jnp.bfloat16

N_ROWS = 24
N_TASK = 32
CHIPS = 384
CHIP_ROWS = 4
WINDOW = 5
OWN = 2
MINE = 6
PAD = 8
SOURCES = 16
HALF_VECTORS = MINE * SOURCES
WIDTH = CHIP_ROWS * TILE


def place(half, y, core):
    z = lax.div(half, 4)
    x = lax.rem(half - z, 4)
    return lax.rem(z, 6) * 4 + x, lax.div(z, 6) * 16 + y * 2 + core


def one_hot(condition):
    return jnp.where(condition, 1.0, 0.0).astype(BF16)


def iota(shape, dim):
    return lax.broadcasted_iota(jnp.int32, shape, dim)


def kernel(
    tiles_ref, meta_ref, info_ref, vec_ref, coef_ref, out_ref,
    send_h, recv_h, send_lab, recv_lab, recv_info, send_v, recv_v,
    band_raw, band, win, total, send_f, recv_f,
    h_send, lab_send, v_send, one_send, rim_send, f_send,
    h_recv, lab_recv, v_recv, info_recv, band_recv, rim_recv, f_recv,
):
    row, task = lax.axis_index("rows"), lax.axis_index("task")
    zh, y, core = lax.div(task, 16), lax.rem(lax.div(task, 2), 8), lax.rem(task, 2)
    z, x = zh * 6 + lax.div(row, 4), lax.rem(row, 4)
    half = 4 * z + lax.rem(x + z, 4)
    chip = half * 8 + y

    def transfer(src, dst, send_sem, recv_sem, where):
        to_row, to_task = where
        here = (to_row == row) & (to_task == task)

        @pl.when(here)
        def _():
            pltpu.make_async_copy(src, dst, recv_sem).start()

        @pl.when(jnp.logical_not(here))
        def _():
            pltpu.make_async_remote_copy(
                src, dst, send_sem, recv_sem, device_id=where, device_id_type=MESH
            ).start()

    def sent(src, send_sem, recv_sem, where):
        to_row, to_task = where

        @pl.when(jnp.logical_not((to_row == row) & (to_task == task)))
        def _():
            pltpu.make_async_remote_copy(
                src, src, send_sem, recv_sem, device_id=where, device_id_type=MESH
            ).wait_send()

    def arrived(buffer, sem):
        pltpu.make_async_copy(buffer, buffer, sem).wait()

    slot_v = zh * 8 + y

    def vector_owner(p):
        return place(2 * row + lax.div(p, 8), lax.rem(p, 8), core)

    mine = vec_ref[...].astype(F32)
    for p in range(SOURCES):
        left = mine[:, p * WIDTH : p * WIDTH + 128]
        right = mine[:, p * WIDTH + 128 : (p + 1) * WIDTH]
        send_v[p] = jnp.concatenate([left, right], axis=0).astype(BF16)

    @pl.loop(0, SOURCES)
    def _(p):
        transfer(send_v.at[p], recv_v.at[slot_v], v_send.at[p], v_recv, vector_owner(p))

    info_owner = place(2 * row + zh, y, core)
    transfer(info_ref, recv_info, one_send.at[0], info_recv, info_owner)

    slots, names = meta_ref[0:1, :], meta_ref[1:2, :]
    place_row = lax.shift_right_logical(iota((N_ROWS * 8, 128), 0), 3)
    pair = [
        jnp.sum(
            jnp.where(slots[:, :128] == (2 * place_row + s) * 8, names[:, :128], 0).astype(F32),
            axis=1,
            keepdims=True,
        )
        for s in range(2)
    ]
    second = (iota((N_ROWS * 8, 128), 1) & 8) > 0
    send_lab[...] = (jnp.where(second, pair[1], pair[0]) - 1.0).reshape(N_ROWS, 8, 128)

    stacked = jnp.concatenate([tiles_ref[:, u * 512 : (u + 1) * 512] for u in range(8)], axis=0)
    packing = one_hot(iota((N_ROWS * 16, 256), 0) == slots)
    packed = jnp.dot(packing, stacked, preferred_element_type=F32)
    send_h[...] = packed.astype(BF16).reshape(N_ROWS, 16, 512)

    def block_owner(to):
        return place(2 * to + zh, y, core)

    @pl.loop(0, N_ROWS)
    def _(k):
        to = lax.rem(row + k, N_ROWS)
        where = block_owner(to)
        transfer(send_lab.at[to], recv_lab.at[row], lab_send.at[to], lab_recv, where)
        transfer(send_h.at[to], recv_h.at[row], h_send.at[to], h_recv, where)

    arrived(recv_v, v_recv)
    pieces = recv_v[...].reshape(SOURCES * 16, 128)

    def selector(shape, vector_dim, side):
        where = iota(shape, 1 - vector_dim)
        lane = where & 7
        vector = lax.shift_right_logical(where, 4) * MINE + lane
        fits = (lane < MINE) & ((where & 8) == 8 * side)
        return one_hot((iota(shape, vector_dim) == vector) & fits)

    for side in range(2):
        pick = selector((HALF_VECTORS, SOURCES * 16), 0, side)
        got = jnp.dot(pick, pieces, preferred_element_type=F32)
        win[0, OWN, :, side * 128 : (side + 1) * 128] = got.astype(BF16)

    def rim(step, away):
        other = lax.rem(chip + away + CHIPS, CHIPS)
        where = place(lax.div(other, 8), lax.rem(other, 8), core)
        index = away + 2 if away < 0 else away + 1
        return pltpu.make_async_remote_copy(
            win.at[step, OWN],
            win.at[step, OWN - away],
            rim_send.at[step, index],
            rim_recv.at[step, OWN - away],
            device_id=where,
            device_id_type=MESH,
        )

    def send_rims(step):
        for away in (-2, 2, -1, 1):
            rim(step, away).start()

    send_rims(0)
    total[...] = coef_ref[0] * win[0, OWN].astype(F32)

    arrived(recv_info, info_recv)
    arrived(recv_lab, lab_recv)
    wide = (N_ROWS * 8, N_ROWS * 16)
    lab = recv_lab[...].reshape(N_ROWS * 8, 128)
    lab = jnp.concatenate([lab] * 3, axis=1)
    keep = iota(wide, 0) == lax.shift_right_logical(iota(wide, 1), 4) * 8
    lab = jnp.sum(jnp.where(keep, lab, 0.0), axis=0, keepdims=True)
    info = jnp.concatenate([recv_info[...]] * 3, axis=1)
    at_slot = iota((32, N_ROWS * 16), 0).astype(F32) == lab
    code = jnp.sum(jnp.where(at_slot, info, 0.0), axis=0, keepdims=True) - 1.0
    goes = code * 8.0 + (iota((1, N_ROWS * 16), 1) & 7).astype(F32)
    columns = WINDOW * CHIP_ROWS
    placing = one_hot(iota((columns * 16, N_ROWS * 16), 0).astype(F32) == goes)

    arrived(recv_h, h_recv)
    blocks = recv_h[...].reshape(N_ROWS * 16, 512)
    raw = jnp.dot(placing, blocks, preferred_element_type=F32)
    low = iota((16, 128), 1) < TILE
    for pair_at in range(columns // 2):
        for group in range(4):
            lanes = slice(group * 128, (group + 1) * 128)
            a = raw[pair_at * 32 : pair_at * 32 + 16, lanes]
            b = raw[pair_at * 32 + 16 : pair_at * 32 + 32, lanes]
            even = jnp.where(low, a, pltpu.roll(b, TILE, 1))
            odd = jnp.where(low, pltpu.roll(a, TILE, 1), b)
            to = slice(pair_at * 128, (pair_at + 1) * 128)
            band_raw[group * 32 : group * 32 + 16, to] = even.astype(BF16)
            band_raw[group * 32 + 16 : group * 32 + 32, to] = odd.astype(BF16)
    at = iota((128, 128), 0)
    inner = lax.shift_right_logical(at, 3) & 7
    source = (at & 7) * 16 + lax.shift_right_logical(at, 6) * 8 + inner
    turn = one_hot(iota((128, 128), 1) == source)
    mine_rows = pl.ds(pl.multiple_of(core * 128, 128), 128)
    band[mine_rows, :] = jnp.dot(turn, band_raw[...], preferred_element_type=F32).astype(BF16)
    sibling = pltpu.make_async_remote_copy(
        band.at[mine_rows],
        band.at[mine_rows],
        one_send.at[1],
        band_recv,
        device_id=(row, task + 1 - 2 * core),
        device_id_type=MESH,
    )
    sibling.start()
    sibling.wait_recv()

    for step in range(ITERS):
        product = None
        for j in (OWN, 1, 3, 0, 4):
            if j != OWN:
                rim(step, OWN - j).wait_recv()
            term = lax.dot_general(
                win[step, j],
                band[:, j * WIDTH : (j + 1) * WIDTH],
                (((1,), (1,)), ((), ())),
                preferred_element_type=F32,
            )
            product = term if product is None else product + term
        if step:
            product = 2.0 * product - win[step - 1, OWN].astype(F32)
        current = product.astype(BF16)
        if step < ITERS - 1:
            win[step + 1, OWN] = current
            send_rims(step + 1)
        total[...] += coef_ref[step + 1] * current.astype(F32)

    result = total[...].astype(BF16)
    spread = None
    for side in range(2):
        put = selector((SOURCES * 16, HALF_VECTORS), 1, side)
        part = jnp.dot(put, result[:, side * 128 : (side + 1) * 128], preferred_element_type=F32)
        spread = part if spread is None else spread + part
    send_f[...] = spread.astype(BF16).reshape(SOURCES, 16, 128)
    slot_f = lax.rem(half, 2) * 8 + y

    def result_owner(q):
        return lax.div(half, 2), lax.div(q, 8) * 16 + lax.rem(q, 8) * 2 + core

    @pl.loop(0, SOURCES)
    def _(q):
        transfer(send_f.at[q], recv_f.at[slot_f], f_send.at[q], f_recv, result_owner(q))

    @pl.loop(0, N_ROWS)
    def _(to):
        where = block_owner(to)
        sent(send_lab.at[to], lab_send.at[to], lab_recv, where)
        sent(send_h.at[to], h_send.at[to], h_recv, where)

    @pl.loop(0, SOURCES)
    def _(p):
        sent(send_v.at[p], v_send.at[p], v_recv, vector_owner(p))
        sent(send_f.at[p], f_send.at[p], f_recv, result_owner(p))

    sent(info_ref, one_send.at[0], info_recv, info_owner)
    sibling.wait_send()
    for step in range(ITERS):
        for away in (-2, 2, -1, 1):
            rim(step, away).wait_send()

    arrived(recv_f, f_recv)
    final = recv_f[...].astype(F32)
    flat = [final[p, 8 * s : 8 * s + 8, :] for p in range(SOURCES) for s in range(2)]
    out_ref[...] = jnp.concatenate(flat, axis=1).astype(BF16)[:MINE, :]


def local(hamiltonian_tiles, tile_target, column_block, row_count, vectors, expansion_coef):
    slots_dev = hamiltonian_tiles.shape[0]
    position = jnp.arange(slots_dev, dtype=jnp.int32)
    owners = tile_target // slots_dev
    earlier = (owners[:, None] == owners[None, :]) & (position[None, :] < position[:, None])
    slot_of = owners * 2 + jnp.sum(earlier.astype(jnp.int32), axis=1)
    slots = (slot_of[None, :] * 8 + jnp.arange(8, dtype=jnp.int32)[:, None]).reshape(1, -1)
    names = jnp.pad(tile_target % slots_dev + 1, (0, 256 - slots_dev))[None, :]
    meta = jnp.concatenate([slots, names], axis=0)
    device = lax.axis_index("rows") * N_TASK + lax.axis_index("task")
    first = (device // 2 - OWN) * CHIP_ROWS
    owner_row = position // SLOTS_ROW
    live = (position % SLOTS_ROW).reshape(2, SLOTS_ROW) < row_count[:, None]
    code = (column_block - first) * 2 + owner_row + 1
    code = jnp.where(live.reshape(-1), code, 0).astype(F32)
    info = jnp.broadcast_to(code[:, None], (slots_dev, 128))
    padded = jnp.pad(vectors, ((0, PAD - MINE), (0, 0)))
    dma = pltpu.SemaphoreType.DMA
    vmem = pl.BlockSpec(memory_space=pltpu.VMEM)
    return pl.pallas_call(
        kernel,
        out_shape=jax.ShapeDtypeStruct(vectors.shape, BF16),
        in_specs=[vmem] * 4 + [pl.BlockSpec(memory_space=pltpu.SMEM)],
        out_specs=vmem,
        scratch_shapes=[
            pltpu.VMEM((N_ROWS, 16, 512), BF16),
            pltpu.VMEM((N_ROWS, 16, 512), BF16),
            pltpu.VMEM((N_ROWS, 8, 128), F32),
            pltpu.VMEM((N_ROWS, 8, 128), F32),
            pltpu.VMEM((32, 128), F32),
            pltpu.VMEM((SOURCES, 16, 128), BF16),
            pltpu.VMEM((SOURCES, 16, 128), BF16),
            pltpu.VMEM((128, WINDOW * WIDTH), BF16),
            pltpu.VMEM((WIDTH, WINDOW * WIDTH), BF16),
            pltpu.VMEM((ITERS, WINDOW, HALF_VECTORS, WIDTH), BF16),
            pltpu.VMEM((HALF_VECTORS, WIDTH), F32),
            pltpu.VMEM((SOURCES, 16, 128), BF16),
            pltpu.VMEM((SOURCES, 16, 128), BF16),
            dma((N_ROWS,)),
            dma((N_ROWS,)),
            dma((SOURCES,)),
            dma((2,)),
            dma((ITERS, 4)),
            dma((SOURCES,)),
            dma(()),
            dma(()),
            dma(()),
            dma(()),
            dma(()),
            dma((ITERS, WINDOW)),
            dma(()),
        ],
        compiler_params=pltpu.CompilerParams(
            has_side_effects=True, vmem_limit_bytes=32 * 1024 * 1024
        ),
    )(hamiltonian_tiles, meta, info, padded, expansion_coef)


def solution(mesh):
    in_specs = (
        P(("rows", "task"), None),
        P(("rows", "task")),
        P(("rows", "task")),
        P(("rows", "task")),
        P("task", "rows"),
        P(),
    )
    out_specs = P("task", "rows")
    return jax.shard_map(local, mesh=mesh, in_specs=in_specs, out_specs=out_specs, check_vma=False)
```

```python
import jax
import jax.numpy as jnp
from jax import lax
from jax.experimental import pallas as pl
from jax.experimental.pallas import tpu as pltpu
from jax.sharding import PartitionSpec as P

TILE = 64
SLOTS_ROW = 16
REACH = 8
ITERS = 4
MESH = pl.DeviceIdType.MESH
F32 = jnp.float32
BF16 = jnp.bfloat16

N_ROWS = 24
N_TASK = 32
CHIPS = 384
CHIP_ROWS = 4
WINDOW = 5
OWN = 2
MINE = 6
PAD = 8
SOURCES = 16
HALF_VECTORS = MINE * SOURCES
GROUPS = 2
PART = HALF_VECTORS // GROUPS
PART_SOURCES = SOURCES // GROUPS
WIDTH = CHIP_ROWS * TILE


def turned(x, z):
    return x + (z & 1) * (3 - 2 * x)


def place(half, y, core):
    z = half >> 2
    x = turned(half & 3, z)
    upper = jnp.where(z >= 6, 1, 0)
    return (z - 6 * upper) * 4 + x, upper * 16 + y * 2 + core


def wrapped(index, size):
    index = jnp.where(index >= size, index - size, index)
    return jnp.where(index < 0, index + size, index)


def one_hot(condition):
    return jnp.where(condition, 1.0, 0.0).astype(BF16)


def iota(shape, dim):
    return lax.broadcasted_iota(jnp.int32, shape, dim)


def kernel(
    tiles_ref, target_ref, column_ref, count_ref, vec_ref, coef_ref, out_ref,
    tiles, send_h, recv_h, send_lab, recv_lab, send_info, recv_info, send_v, recv_v,
    band_raw, band, win, total, send_f, recv_f,
    h_send, lab_send, v_send, one_send, rim_send, f_send,
    load, h_recv, lab_recv, v_recv, info_recv, band_recv, rim_recv, f_recv,
):
    row, task = lax.axis_index("rows"), lax.axis_index("task")
    zh, y, core = task >> 4, (task >> 1) & 7, task & 1
    z, x = zh * 6 + (row >> 2), row & 3
    half = 4 * z + turned(x, z)
    chip = half * 8 + y

    def is_here(where):
        return (where[0] == row) & (where[1] == task)

    def transfer(src, dst, send_sem, recv_sem, where):
        here = is_here(where)

        @pl.when(here)
        def _():
            pltpu.make_async_copy(src, dst, recv_sem).start()

        @pl.when(jnp.logical_not(here))
        def _():
            pltpu.make_async_remote_copy(
                src, dst, send_sem, recv_sem, device_id=where, device_id_type=MESH
            ).start()

    def sent(src, send_sem, recv_sem, where):
        @pl.when(jnp.logical_not(is_here(where)))
        def _():
            pltpu.make_async_remote_copy(
                src, src, send_sem, recv_sem, device_id=where, device_id_type=MESH
            ).wait_send()

    def arrived(buffer, sem):
        pltpu.make_async_copy(buffer, buffer, sem).wait()

    def vector_owner(p):
        return place(2 * row + (p >> 3), p & 7, core)

    def vector_home(q):
        return half >> 1, (q >> 3) * 16 + (q & 7) * 2 + core

    def block_owner(to):
        return place(2 * to + zh, y, core)

    def rim_owner(away):
        other = wrapped(chip + away, CHIPS)
        return place(other >> 3, other & 7, core)

    load_tiles = pltpu.make_async_copy(tiles_ref, tiles, load)
    load_tiles.start()
    recv_lab[...] = jnp.zeros(recv_lab.shape, F32)

    barrier = pltpu.get_barrier_semaphore()

    def greet(where):
        @pl.when(jnp.logical_not(is_here(where)))
        def _():
            pl.semaphore_signal(barrier, inc=1, device_id=where, device_id_type=MESH)

    @pl.loop(0, SOURCES)
    def _(p):
        greet(vector_home(p))
        greet(vector_owner(p))

    @pl.loop(0, N_ROWS)
    def _(source):
        greet((source, (half & 1) * 16 + y * 2 + core))

    for away in (-2, 2, -1, 1):
        greet(rim_owner(away))
    greet((row, task + 1 - 2 * core))

    mine = vec_ref[...].astype(F32)
    for p in range(SOURCES):
        left = mine[:, p * WIDTH : p * WIDTH + 128]
        right = mine[:, p * WIDTH + 128 : (p + 1) * WIDTH]
        send_v[p] = jnp.concatenate([left, right], axis=0).astype(BF16)

    lane = iota((1, 32), 1)
    second_row = lane >> 4
    first = ((row * N_TASK + task) >> 1) * CHIP_ROWS - OWN * CHIP_ROWS
    live = (lane & 15) < jnp.where(second_row == 1, count_ref[0, 1], count_ref[0, 0])
    code = jnp.where(live, (column_ref[...] - first) * 2 + second_row + 1, 0)
    send_info[...] = jnp.zeros(send_info.shape, F32)
    send_info[0:1, 0:32] = code.astype(F32)

    target = target_ref[...]
    diagonal = iota((32, 32), 0) == iota((32, 32), 1)
    as_column = jnp.sum(jnp.where(diagonal, target, 0).astype(F32), axis=1, keepdims=True)
    as_column = as_column.astype(jnp.int32)
    owner_column, name_column = as_column >> 5, as_column & 31
    owner_row = target >> 5
    earlier = (owner_column == owner_row) & (iota((32, 32), 1) < iota((32, 32), 0))
    rank = jnp.sum(jnp.where(earlier, 1.0, 0.0), axis=1, keepdims=True)
    slot = (owner_column.astype(F32) * 2.0 + rank) * 8.0
    spread = (iota((32, 256), 1) & 31) == iota((32, 256), 0)
    slots = jnp.sum(jnp.where(spread, slot, 0.0), axis=0, keepdims=True)
    slots = slots.astype(jnp.int32) + (iota((1, 256), 1) >> 5)

    goes_to = one_hot(owner_row == (iota((N_ROWS * 8, 32), 0) >> 3))
    which = ((iota((32, 128), 1) >> 3) & 1).astype(F32) == rank
    named = jnp.where(which, (name_column + 1).astype(F32), 0.0).astype(BF16)
    names = jnp.dot(goes_to, named, preferred_element_type=F32) - 1.0
    send_lab[...] = names.reshape(N_ROWS, 8, 128)

    load_tiles.wait()
    stacked = jnp.concatenate([tiles[:, u * 512 : (u + 1) * 512] for u in range(8)], axis=0)
    packing = one_hot(iota((N_ROWS * 16, 256), 0) == slots)
    packed = jnp.dot(packing, stacked, preferred_element_type=F32)
    send_h[...] = packed.astype(BF16).reshape(N_ROWS, 16, 512)

    to_self = jnp.where((half & 1) == zh, 1, 0) + 2 * jnp.where((half >> 1) == row, 1, 0)
    pl.semaphore_wait(barrier, N_ROWS + 2 * SOURCES + 5 - to_self)

    slot_v = zh * 8 + y
    one_line = pl.ds(0, 1)
    info_owner = place(2 * row + zh, y, core)

    @pl.loop(0, SOURCES)
    def _(p):
        where = vector_owner(p)
        transfer(send_v.at[p], recv_v.at[slot_v], v_send.at[p], v_recv.at[zh], where)

    transfer(send_info.at[one_line], recv_info.at[one_line], one_send.at[0], info_recv, info_owner)

    @pl.loop(0, N_ROWS)
    def _(k):
        level = k >> 1
        far = 6 - ((level + 1) >> 1)
        there = wrapped(z + far * (2 * (level & 1) - 1), 12)
        to = 2 * there + (k & 1)
        where = block_owner(to)
        transfer(
            send_lab.at[to, one_line], recv_lab.at[row, one_line], lab_send.at[to], lab_recv, where
        )
        transfer(send_h.at[to], recv_h.at[row], h_send.at[to], h_recv, where)

    def selector(shape, vector_dim, side):
        where = iota(shape, 1 - vector_dim)
        at = where & 7
        vector = (where >> 4) * MINE + at
        fits = (at < MINE) & ((where & 8) == 8 * side)
        return one_hot((iota(shape, vector_dim) == vector) & fits)

    def rim(step, part, away):
        index = away + 2 if away < 0 else away + 1
        rows = pl.ds(part * PART, PART)
        return pltpu.make_async_remote_copy(
            win.at[step, OWN, rows],
            win.at[step, OWN - away, rows],
            rim_send.at[step, part, index],
            rim_recv.at[step, part, OWN - away],
            device_id=rim_owner(away),
            device_id_type=MESH,
        )

    def send_rims(step, part):
        for away in (-2, 2, -1, 1):
            rim(step, part, away).start()

    def rows_of(part):
        return slice(part * PART, (part + 1) * PART)

    for part in range(GROUPS):
        sources = pl.ds(part * PART_SOURCES, PART_SOURCES)
        arrived(recv_v.at[sources], v_recv.at[part])
        pieces = recv_v[sources].reshape(PART_SOURCES * 16, 128)
        for side in range(2):
            pick = selector((PART, PART_SOURCES * 16), 0, side)
            got = jnp.dot(pick, pieces, preferred_element_type=F32)
            win[0, OWN, rows_of(part), side * 128 : (side + 1) * 128] = got.astype(BF16)
        send_rims(0, part)
    total[...] = coef_ref[0] * win[0, OWN].astype(F32)

    arrived(recv_info.at[one_line], info_recv)
    arrived(recv_lab.at[:, one_line], lab_recv)
    wide = (N_ROWS * 8, N_ROWS * 16)
    lab = recv_lab[...].reshape(N_ROWS * 8, 128)
    lab = jnp.concatenate([lab] * 3, axis=1)
    keep = iota(wide, 0) == (iota(wide, 1) >> 4) * 8
    lab = jnp.sum(jnp.where(keep, lab, 0.0), axis=0, keepdims=True)
    on_diagonal = iota((32, 128), 0) == iota((32, 128), 1)
    info = jnp.sum(jnp.where(on_diagonal, recv_info[0:1, :], 0.0), axis=1, keepdims=True)
    at_slot = iota((32, N_ROWS * 16), 0).astype(F32) == lab
    code = jnp.sum(jnp.where(at_slot, info, 0.0), axis=0, keepdims=True) - 1.0
    goes = code * 8.0 + (iota((1, N_ROWS * 16), 1) & 7).astype(F32)
    columns = WINDOW * CHIP_ROWS
    placing = one_hot(iota((columns * 16, N_ROWS * 16), 0).astype(F32) == goes)
    at = iota((128, 128), 0)
    source = (at & 7) * 16 + (at >> 6) * 8 + ((at >> 3) & 7)
    turn = one_hot(iota((128, 128), 1) == source)

    arrived(recv_h, h_recv)
    blocks = recv_h[...].reshape(N_ROWS * 16, 512)
    raw = jnp.dot(placing, blocks, preferred_element_type=F32)
    low = iota((16, 128), 1) < TILE
    for pair_at in range(columns // 2):
        for group in range(4):
            lanes = slice(group * 128, (group + 1) * 128)
            a = raw[pair_at * 32 : pair_at * 32 + 16, lanes]
            b = raw[pair_at * 32 + 16 : pair_at * 32 + 32, lanes]
            even = jnp.where(low, a, pltpu.roll(b, TILE, 1))
            odd = jnp.where(low, pltpu.roll(a, TILE, 1), b)
            to = slice(pair_at * 128, (pair_at + 1) * 128)
            band_raw[group * 32 : group * 32 + 16, to] = even.astype(BF16)
            band_raw[group * 32 + 16 : group * 32 + 32, to] = odd.astype(BF16)
    mine_rows = pl.ds(pl.multiple_of(core * 128, 128), 128)
    band[mine_rows, :] = jnp.dot(turn, band_raw[...], preferred_element_type=F32).astype(BF16)
    sibling = pltpu.make_async_remote_copy(
        band.at[mine_rows],
        band.at[mine_rows],
        one_send.at[1],
        band_recv,
        device_id=(row, task + 1 - 2 * core),
        device_id_type=MESH,
    )
    sibling.start()
    sibling.wait_recv()

    slot_f = (half & 1) * 8 + y
    for step in range(ITERS):
        for part in range(GROUPS):
            rows = rows_of(part)
            product = None
            for j in (OWN, 1, 3, 0, 4):
                if j != OWN:
                    rim(step, part, OWN - j).wait_recv()
                term = lax.dot_general(
                    win[step, j, rows],
                    band[:, j * WIDTH : (j + 1) * WIDTH],
                    (((1,), (1,)), ((), ())),
                    preferred_element_type=F32,
                )
                product = term if product is None else product + term
            if step:
                product = 2.0 * product - win[step - 1, OWN, rows].astype(F32)
            current = product.astype(BF16)
            if step < ITERS - 1:
                win[step + 1, OWN, rows] = current
                send_rims(step + 1, part)
                total[rows] += coef_ref[step + 1] * current.astype(F32)
                continue
            result = (total[rows] + coef_ref[step + 1] * current.astype(F32)).astype(BF16)
            spread = None
            for side in range(2):
                put = selector((PART_SOURCES * 16, PART), 1, side)
                half_result = result[:, side * 128 : (side + 1) * 128]
                term = jnp.dot(put, half_result, preferred_element_type=F32)
                spread = term if spread is None else spread + term
            sources = slice(part * PART_SOURCES, (part + 1) * PART_SOURCES)
            send_f[sources] = spread.astype(BF16).reshape(PART_SOURCES, 16, 128)

            @pl.loop(part * PART_SOURCES, (part + 1) * PART_SOURCES)
            def _(q):
                where = vector_home(q)
                transfer(send_f.at[q], recv_f.at[slot_f], f_send.at[q], f_recv, where)

    @pl.loop(0, N_ROWS)
    def _(to):
        where = block_owner(to)
        sent(send_lab.at[to, one_line], lab_send.at[to], lab_recv, where)
        sent(send_h.at[to], h_send.at[to], h_recv, where)

    @pl.loop(0, SOURCES)
    def _(p):
        sent(send_v.at[p], v_send.at[p], v_recv.at[zh], vector_owner(p))
        sent(send_f.at[p], f_send.at[p], f_recv, vector_home(p))

    sent(send_info.at[one_line], one_send.at[0], info_recv, info_owner)
    sibling.wait_send()
    for step in range(ITERS):
        for part in range(GROUPS):
            for away in (-2, 2, -1, 1):
                rim(step, part, away).wait_send()

    arrived(recv_f, f_recv)
    final = recv_f[...].astype(F32)
    flat = [final[p, 8 * s : 8 * s + 8, :] for p in range(SOURCES) for s in range(2)]
    out_ref[...] = jnp.concatenate(flat, axis=1).astype(BF16)[:MINE, :]


def local(hamiltonian_tiles, tile_target, column_block, row_count, vectors, expansion_coef):
    padded = jnp.pad(vectors, ((0, PAD - MINE), (0, 0)))
    dma = pltpu.SemaphoreType.DMA
    vmem = pl.BlockSpec(memory_space=pltpu.VMEM)
    smem = pl.BlockSpec(memory_space=pltpu.SMEM)
    return pl.pallas_call(
        kernel,
        out_shape=jax.ShapeDtypeStruct(vectors.shape, BF16),
        in_specs=[pl.BlockSpec(memory_space=pl.ANY), vmem, vmem, smem, vmem, smem],
        out_specs=vmem,
        scratch_shapes=[
            pltpu.VMEM((32, TILE * TILE), BF16),
            pltpu.VMEM((N_ROWS, 16, 512), BF16),
            pltpu.VMEM((N_ROWS, 16, 512), BF16),
            pltpu.VMEM((N_ROWS, 8, 128), F32),
            pltpu.VMEM((N_ROWS, 8, 128), F32),
            pltpu.VMEM((8, 128), F32),
            pltpu.VMEM((8, 128), F32),
            pltpu.VMEM((SOURCES, 16, 128), BF16),
            pltpu.VMEM((SOURCES, 16, 128), BF16),
            pltpu.VMEM((128, WINDOW * WIDTH), BF16),
            pltpu.VMEM((WIDTH, WINDOW * WIDTH), BF16),
            pltpu.VMEM((ITERS, WINDOW, HALF_VECTORS, WIDTH), BF16),
            pltpu.VMEM((HALF_VECTORS, WIDTH), F32),
            pltpu.VMEM((SOURCES, 16, 128), BF16),
            pltpu.VMEM((SOURCES, 16, 128), BF16),
            dma((N_ROWS,)),
            dma((N_ROWS,)),
            dma((SOURCES,)),
            dma((2,)),
            dma((ITERS, GROUPS, 4)),
            dma((SOURCES,)),
            dma(()),
            dma(()),
            dma(()),
            dma((GROUPS,)),
            dma(()),
            dma(()),
            dma((ITERS, GROUPS, WINDOW)),
            dma(()),
        ],
        compiler_params=pltpu.CompilerParams(
            collective_id=0, has_side_effects=True, vmem_limit_bytes=32 * 1024 * 1024
        ),
    )(
        hamiltonian_tiles,
        tile_target[None, :],
        column_block[None, :],
        row_count[None, :],
        padded,
        expansion_coef,
    )


def solution(mesh):
    in_specs = (
        P(("rows", "task"), None),
        P(("rows", "task")),
        P(("rows", "task")),
        P(("rows", "task")),
        P("task", "rows"),
        P(),
    )
    out_specs = P("task", "rows")
    return jax.shard_map(local, mesh=mesh, in_specs=in_specs, out_specs=out_specs, check_vma=False)
```

```python
import jax
import jax.numpy as jnp
from jax import lax
from jax.experimental import pallas as pl
from jax.experimental.pallas import tpu as pltpu
from jax.sharding import PartitionSpec as P

TILE = 64
SLOTS_ROW = 16
REACH = 8
ITERS = 4
MESH = pl.DeviceIdType.MESH
F32 = jnp.float32
BF16 = jnp.bfloat16

N_ROWS = 24
N_TASK = 32
CHIPS = 384
LEVELS = 12
CHIP_ROWS = 4
WINDOW = 5
OWN = 2
MINE = 6
PAD = 8
SOURCES = 16
HALF_VECTORS = MINE * SOURCES
GROUPS = 3
PART = HALF_VECTORS // GROUPS
WIDTH = CHIP_ROWS * TILE


def turned(x, z):
    return x + (z & 1) * (3 - 2 * x)


def farthest_first(k, size):
    return (size // 2 - ((k + 1) >> 1)) * (2 * (k & 1) - 1)


def along(at, half):
    return at + (half & 1) * (7 - 2 * at)


def place(half, at, core):
    z = half >> 2
    x = turned(half & 3, z)
    upper = jnp.where(z >= 6, 1, 0)
    return (z - 6 * upper) * 4 + x, upper * 16 + along(at, half) * 2 + core


def wrapped(index, size):
    index = jnp.where(index >= size, index - size, index)
    return jnp.where(index < 0, index + size, index)


def one_hot(condition):
    return jnp.where(condition, 1.0, 0.0).astype(BF16)


def iota(shape, dim):
    return lax.broadcasted_iota(jnp.int32, shape, dim)


def kernel(
    tiles_ref, target_ref, column_ref, count_ref, vec_ref, coef_ref, out_ref,
    tiles, vec, padded, send_h, recv_h, send_lab, recv_lab, send_info, recv_info, send_v, recv_v,
    band_raw, band, win, total, results, send_f, recv_f,
    h_send, lab_send, v_send, one_send, rim_send, f_send,
    load, h_recv, lab_recv, v_recv, info_recv, band_recv, rim_recv, f_recv,
):
    row, task = lax.axis_index("rows"), lax.axis_index("task")
    zh, y, core = task >> 4, (task >> 1) & 7, task & 1
    z, x = zh * 6 + (row >> 2), row & 3
    half = 4 * z + turned(x, z)
    at = along(y, half)
    chip = half * 8 + at

    def is_here(where):
        return (where[0] == row) & (where[1] == task)

    def transfer(src, dst, send_sem, recv_sem, where):
        here = is_here(where)

        @pl.when(here)
        def _():
            pltpu.make_async_copy(src, dst, recv_sem).start()

        @pl.when(jnp.logical_not(here))
        def _():
            pltpu.make_async_remote_copy(
                src, dst, send_sem, recv_sem, device_id=where, device_id_type=MESH
            ).start()

    def sent(src, send_sem, recv_sem, where):
        @pl.when(jnp.logical_not(is_here(where)))
        def _():
            pltpu.make_async_remote_copy(
                src, src, send_sem, recv_sem, device_id=where, device_id_type=MESH
            ).wait_send()

    def arrived(buffer, sem):
        pltpu.make_async_copy(buffer, buffer, sem).wait()

    def vector_owner(p):
        return place(2 * row + (p >> 3), p & 7, core)

    def vector_home(q):
        return half >> 1, (q >> 3) * 16 + (q & 7) * 2 + core

    def block_owner(to):
        return place(2 * to + zh, y, core)

    def rim_owner(away):
        other = wrapped(chip + away, CHIPS)
        return place(other >> 3, other & 7, core)

    load_tiles = pltpu.make_async_copy(tiles_ref, tiles, load.at[0])
    load_tiles.start()
    load_vec = pltpu.make_async_copy(vec_ref, vec, load.at[1])
    load_vec.start()
    recv_lab[...] = jnp.zeros(recv_lab.shape, F32)

    barrier = pltpu.get_barrier_semaphore()

    def greet(where):
        @pl.when(jnp.logical_not(is_here(where)))
        def _():
            pl.semaphore_signal(barrier, inc=1, device_id=where, device_id_type=MESH)

    @pl.loop(0, N_ROWS)
    def _(source):
        greet((source, (half & 1) * 16 + at * 2 + core))

    @pl.loop(0, SOURCES)
    def _(p):
        greet(vector_home(p))
        greet(vector_owner(p))

    for away in (-2, 2, -1, 1):
        greet(rim_owner(away))
    greet((row, task + 1 - 2 * core))

    load_vec.wait()
    padded[...] = jnp.zeros(padded.shape, F32)
    padded[:MINE, :] = vec[...].astype(F32)
    mine = padded[...]
    for p in range(SOURCES):
        left = mine[:, p * WIDTH : p * WIDTH + 128]
        right = mine[:, p * WIDTH + 128 : (p + 1) * WIDTH]
        send_v[p] = jnp.concatenate([left, right], axis=0).astype(BF16)

    lane = iota((1, 32), 1)
    second_row = lane >> 4
    first = ((row * N_TASK + task) >> 1) * CHIP_ROWS - OWN * CHIP_ROWS
    live = (lane & 15) < jnp.where(second_row == 1, count_ref[0, 1], count_ref[0, 0])
    code = jnp.where(live, (column_ref[...] - first) * 2 + second_row + 1, 0)
    send_info[...] = jnp.zeros(send_info.shape, F32)
    send_info[0:1, 0:32] = code.astype(F32)

    target = target_ref[...]
    diagonal = iota((32, 32), 0) == iota((32, 32), 1)
    as_column = jnp.sum(jnp.where(diagonal, target, 0).astype(F32), axis=1, keepdims=True)
    as_column = as_column.astype(jnp.int32)
    owner_column, name_column = as_column >> 5, as_column & 31
    owner_row = target >> 5
    earlier = (owner_column == owner_row) & (iota((32, 32), 1) < iota((32, 32), 0))
    rank = jnp.sum(jnp.where(earlier, 1.0, 0.0), axis=1, keepdims=True)
    slot = (owner_column.astype(F32) * 2.0 + rank) * 8.0
    spread = (iota((32, 256), 1) & 31) == iota((32, 256), 0)
    slots = jnp.sum(jnp.where(spread, slot, 0.0), axis=0, keepdims=True)
    slots = slots.astype(jnp.int32) + (iota((1, 256), 1) >> 5)

    goes_to = one_hot(owner_row == (iota((N_ROWS * 8, 32), 0) >> 3))
    which = ((iota((32, 128), 1) >> 3) & 1).astype(F32) == rank
    named = jnp.where(which, (name_column + 1).astype(F32), 0.0).astype(BF16)
    names = jnp.dot(goes_to, named, preferred_element_type=F32) - 1.0
    send_lab[...] = names.reshape(N_ROWS, 8, 128)

    load_tiles.wait()
    stacked = jnp.concatenate([tiles[:, u * 512 : (u + 1) * 512] for u in range(8)], axis=0)
    packing = one_hot(iota((N_ROWS * 16, 256), 0) == slots)
    packed = jnp.dot(packing, stacked, preferred_element_type=F32)
    send_h[...] = packed.astype(BF16).reshape(N_ROWS, 16, 512)

    to_self = jnp.where(((half & 1) == zh) & (at == y), 1, 0) + 2 * jnp.where((half >> 1) == row, 1, 0)
    pl.semaphore_wait(barrier, N_ROWS + 2 * SOURCES + 5 - to_self)

    slot_v = zh * 8 + y
    one_line = pl.ds(0, 1)
    info_owner = place(2 * row + zh, y, core)

    @pl.loop(0, SOURCES)
    def _(k):
        p = (k & 1) * 8 + ((y + farthest_first(k >> 1, 8)) & 7)
        transfer(send_v.at[p], recv_v.at[slot_v], v_send.at[p], v_recv, vector_owner(p))

    transfer(send_info.at[one_line], recv_info.at[one_line], one_send.at[0], info_recv, info_owner)

    @pl.loop(0, N_ROWS)
    def _(k):
        there = wrapped(z + farthest_first(k >> 1, LEVELS), LEVELS)
        to = 2 * there + (k & 1)
        where = block_owner(to)
        transfer(
            send_lab.at[to, one_line], recv_lab.at[row, one_line], lab_send.at[to], lab_recv, where
        )
        transfer(send_h.at[to], recv_h.at[row], h_send.at[to], h_recv, where)

    def selector(shape, vector_dim, side, source=0):
        where = iota(shape, 1 - vector_dim)
        lane = where & 7
        vector = ((where >> 4) + source) * MINE + lane
        fits = (lane < MINE) & ((where & 8) == 8 * side)
        return one_hot((iota(shape, vector_dim) == vector) & fits)

    def rim(step, part, away):
        index = away + 2 if away < 0 else away + 1
        rows = pl.ds(part * PART, PART)
        return pltpu.make_async_remote_copy(
            win.at[step, OWN, rows],
            win.at[step, OWN - away, rows],
            rim_send.at[step, part, index],
            rim_recv.at[step, part, OWN - away],
            device_id=rim_owner(away),
            device_id_type=MESH,
        )

    def send_rims(step, part):
        for away in (-2, 2, -1, 1):
            rim(step, part, away).start()

    def rows_of(part):
        return slice(part * PART, (part + 1) * PART)

    arrived(recv_v, v_recv)
    pieces = recv_v[...].reshape(SOURCES * 16, 128)
    for side in range(2):
        pick = selector((HALF_VECTORS, SOURCES * 16), 0, side)
        got = jnp.dot(pick, pieces, preferred_element_type=F32)
        win[0, OWN, :, side * 128 : (side + 1) * 128] = got.astype(BF16)
    for part in range(GROUPS):
        send_rims(0, part)
    total[...] = coef_ref[0] * win[0, OWN].astype(F32)

    arrived(recv_info.at[one_line], info_recv)
    arrived(recv_lab.at[:, one_line], lab_recv)
    wide = (N_ROWS * 8, N_ROWS * 16)
    lab = recv_lab[...].reshape(N_ROWS * 8, 128)
    lab = jnp.concatenate([lab] * 3, axis=1)
    keep = iota(wide, 0) == (iota(wide, 1) >> 4) * 8
    lab = jnp.sum(jnp.where(keep, lab, 0.0), axis=0, keepdims=True)
    on_diagonal = iota((32, 128), 0) == iota((32, 128), 1)
    info = jnp.sum(jnp.where(on_diagonal, recv_info[0:1, :], 0.0), axis=1, keepdims=True)
    at_slot = iota((32, N_ROWS * 16), 0).astype(F32) == lab
    code = jnp.sum(jnp.where(at_slot, info, 0.0), axis=0, keepdims=True) - 1.0
    goes = code * 8.0 + (iota((1, N_ROWS * 16), 1) & 7).astype(F32)
    columns = WINDOW * CHIP_ROWS
    placing = one_hot(iota((columns * 16, N_ROWS * 16), 0).astype(F32) == goes)
    line = iota((128, 128), 0)
    source = (line & 7) * 16 + (line >> 6) * 8 + ((line >> 3) & 7)
    turn = one_hot(iota((128, 128), 1) == source)

    arrived(recv_h, h_recv)
    blocks = recv_h[...].reshape(N_ROWS * 16, 512)
    raw = jnp.dot(placing, blocks, preferred_element_type=F32)
    low = iota((16, 128), 1) < TILE
    for pair_at in range(columns // 2):
        for group in range(4):
            lanes = slice(group * 128, (group + 1) * 128)
            a = raw[pair_at * 32 : pair_at * 32 + 16, lanes]
            b = raw[pair_at * 32 + 16 : pair_at * 32 + 32, lanes]
            even = jnp.where(low, a, pltpu.roll(b, TILE, 1))
            odd = jnp.where(low, pltpu.roll(a, TILE, 1), b)
            to = slice(pair_at * 128, (pair_at + 1) * 128)
            band_raw[group * 32 : group * 32 + 16, to] = even.astype(BF16)
            band_raw[group * 32 + 16 : group * 32 + 32, to] = odd.astype(BF16)
    mine_rows = pl.ds(pl.multiple_of(core * 128, 128), 128)
    band[mine_rows, :] = jnp.dot(turn, band_raw[...], preferred_element_type=F32).astype(BF16)
    sibling = pltpu.make_async_remote_copy(
        band.at[mine_rows],
        band.at[mine_rows],
        one_send.at[1],
        band_recv,
        device_id=(row, task + 1 - 2 * core),
        device_id_type=MESH,
    )
    sibling.start()
    sibling.wait_recv()

    slot_f = (half & 1) * 8 + at
    for step in range(ITERS):
        for part in range(GROUPS):
            rows = rows_of(part)
            product = None
            for j in (OWN, 1, 3, 0, 4):
                if j != OWN:
                    rim(step, part, OWN - j).wait_recv()
                term = lax.dot_general(
                    win[step, j, rows],
                    band[:, j * WIDTH : (j + 1) * WIDTH],
                    (((1,), (1,)), ((), ())),
                    preferred_element_type=F32,
                )
                product = term if product is None else product + term
            if step:
                product = 2.0 * product - win[step - 1, OWN, rows].astype(F32)
            current = product.astype(BF16)
            if step < ITERS - 1:
                win[step + 1, OWN, rows] = current
                send_rims(step + 1, part)
                total[rows] += coef_ref[step + 1] * current.astype(F32)
                continue
            result = total[rows] + coef_ref[step + 1] * current.astype(F32)
            results[rows, :] = result.astype(BF16)
            begin, end = part * PART // MINE, (part + 1) * PART // MINE
            spread = None
            for side in range(2):
                put = selector(((end - begin) * 16, (part + 1) * PART), 1, side, begin)
                ready = results[: (part + 1) * PART, side * 128 : (side + 1) * 128]
                term = jnp.dot(put, ready, preferred_element_type=F32)
                spread = term if spread is None else spread + term
            send_f[begin:end] = spread.astype(BF16).reshape(end - begin, 16, 128)

            @pl.loop(begin, end)
            def _(q):
                where = vector_home(q)
                transfer(send_f.at[q], recv_f.at[slot_f], f_send.at[q], f_recv, where)

    @pl.loop(0, N_ROWS)
    def _(to):
        where = block_owner(to)
        sent(send_lab.at[to, one_line], lab_send.at[to], lab_recv, where)
        sent(send_h.at[to], h_send.at[to], h_recv, where)

    @pl.loop(0, SOURCES)
    def _(p):
        sent(send_v.at[p], v_send.at[p], v_recv, vector_owner(p))
        sent(send_f.at[p], f_send.at[p], f_recv, vector_home(p))

    sent(send_info.at[one_line], one_send.at[0], info_recv, info_owner)
    sibling.wait_send()
    for step in range(ITERS):
        for part in range(GROUPS):
            for away in (-2, 2, -1, 1):
                rim(step, part, away).wait_send()

    arrived(recv_f, f_recv)
    final = recv_f[...].astype(F32)
    flat = [final[p, 8 * s : 8 * s + 8, :] for p in range(SOURCES) for s in range(2)]
    out_ref[...] = jnp.concatenate(flat, axis=1).astype(BF16)[:MINE, :]


def local(hamiltonian_tiles, tile_target, column_block, row_count, vectors, expansion_coef):
    dma = pltpu.SemaphoreType.DMA
    vmem = pl.BlockSpec(memory_space=pltpu.VMEM)
    anywhere = pl.BlockSpec(memory_space=pl.ANY)
    smem = pl.BlockSpec(memory_space=pltpu.SMEM)
    return pl.pallas_call(
        kernel,
        out_shape=jax.ShapeDtypeStruct(vectors.shape, BF16),
        in_specs=[anywhere, vmem, vmem, smem, anywhere, smem],
        out_specs=vmem,
        scratch_shapes=[
            pltpu.VMEM((32, TILE * TILE), BF16),
            pltpu.VMEM(vectors.shape, BF16),
            pltpu.VMEM((PAD, vectors.shape[1]), F32),
            pltpu.VMEM((N_ROWS, 16, 512), BF16),
            pltpu.VMEM((N_ROWS, 16, 512), BF16),
            pltpu.VMEM((N_ROWS, 8, 128), F32),
            pltpu.VMEM((N_ROWS, 8, 128), F32),
            pltpu.VMEM((8, 128), F32),
            pltpu.VMEM((8, 128), F32),
            pltpu.VMEM((SOURCES, 16, 128), BF16),
            pltpu.VMEM((SOURCES, 16, 128), BF16),
            pltpu.VMEM((128, WINDOW * WIDTH), BF16),
            pltpu.VMEM((WIDTH, WINDOW * WIDTH), BF16),
            pltpu.VMEM((ITERS, WINDOW, HALF_VECTORS, WIDTH), BF16),
            pltpu.VMEM((HALF_VECTORS, WIDTH), F32),
            pltpu.VMEM((HALF_VECTORS, WIDTH), BF16),
            pltpu.VMEM((SOURCES, 16, 128), BF16),
            pltpu.VMEM((SOURCES, 16, 128), BF16),
            dma((N_ROWS,)),
            dma((N_ROWS,)),
            dma((SOURCES,)),
            dma((2,)),
            dma((ITERS, GROUPS, 4)),
            dma((SOURCES,)),
            dma((2,)),
            dma(()),
            dma(()),
            dma(()),
            dma(()),
            dma(()),
            dma((ITERS, GROUPS, WINDOW)),
            dma(()),
        ],
        compiler_params=pltpu.CompilerParams(
            collective_id=0, has_side_effects=True, vmem_limit_bytes=60 * 1024 * 1024
        ),
    )(
        hamiltonian_tiles,
        tile_target[None, :],
        column_block[None, :],
        row_count[None, :],
        vectors,
        expansion_coef,
    )


def solution(mesh):
    in_specs = (
        P(("rows", "task"), None),
        P(("rows", "task")),
        P(("rows", "task")),
        P(("rows", "task")),
        P("task", "rows"),
        P(),
    )
    out_specs = P("task", "rows")
    return jax.shard_map(local, mesh=mesh, in_specs=in_specs, out_specs=out_specs, check_vma=False)
```

```python
import jax
import jax.numpy as jnp
from jax import lax
from jax.experimental import pallas as pl
from jax.experimental.pallas import tpu as pltpu
from jax.sharding import PartitionSpec as P

TILE = 64
SLOTS_ROW = 16
REACH = 8
ITERS = 4
MESH = pl.DeviceIdType.MESH
F32 = jnp.float32
BF16 = jnp.bfloat16

N_ROWS = 24
N_TASK = 32
CHIPS = 384
LEVELS = 12
CHIP_ROWS = 4
WINDOW = 5
OWN = 2
MINE = 6
PAD = 8
SOURCES = 16
HALF_VECTORS = MINE * SOURCES
GROUPS = 3
PART = HALF_VECTORS // GROUPS
WIDTH = CHIP_ROWS * TILE


def turned(x, z):
    return x + (z & 1) * (3 - 2 * x)


def farthest_first(k, size):
    return (size // 2 - ((k + 1) >> 1)) * (2 * (k & 1) - 1)


def along(at, half):
    return at + (half & 1) * (7 - 2 * at)


def place(half, at, core):
    z = half >> 2
    x = turned(half & 3, z)
    upper = jnp.where(z >= 6, 1, 0)
    return (z - 6 * upper) * 4 + x, upper * 16 + along(at, half) * 2 + core


def wrapped(index, size):
    index = jnp.where(index >= size, index - size, index)
    return jnp.where(index < 0, index + size, index)


def one_hot(condition):
    return jnp.where(condition, 1.0, 0.0).astype(BF16)


def iota(shape, dim):
    return lax.broadcasted_iota(jnp.int32, shape, dim)


def kernel(
    tiles_ref, target_ref, column_ref, count_ref, vec_ref, coef_ref, out_ref,
    tiles, target, column, count, vec, coef, padded, send_h, recv_h, send_lab, recv_lab, send_info, recv_info, send_v, recv_v,
    band_raw, band, win, total, results, send_f, recv_f,
    h_send, lab_send, v_send, one_send, rim_send, f_send,
    load, h_recv, lab_recv, v_recv, info_recv, band_recv, rim_recv, f_recv,
):
    row, task = lax.axis_index("rows"), lax.axis_index("task")
    zh, y, core = task >> 4, (task >> 1) & 7, task & 1
    z, x = zh * 6 + (row >> 2), row & 3
    half = 4 * z + turned(x, z)
    at = along(y, half)
    chip = half * 8 + at

    def is_here(where):
        return (where[0] == row) & (where[1] == task)

    def transfer(src, dst, send_sem, recv_sem, where):
        here = is_here(where)

        @pl.when(here)
        def _():
            pltpu.make_async_copy(src, dst, recv_sem).start()

        @pl.when(jnp.logical_not(here))
        def _():
            pltpu.make_async_remote_copy(
                src, dst, send_sem, recv_sem, device_id=where, device_id_type=MESH
            ).start()

    def arrived(buffer, sem):
        pltpu.make_async_copy(buffer, buffer, sem).wait()

    def sent(buffer, sem, one_stays):
        @pl.when(one_stays)
        def _():
            arrived(buffer.at[pl.ds(1, buffer.shape[0] - 1)], sem)

        @pl.when(jnp.logical_not(one_stays))
        def _():
            arrived(buffer, sem)

    def vector_owner(p):
        return place(2 * row + (p >> 3), p & 7, core)

    def vector_home(q):
        return half >> 1, (q >> 3) * 16 + (q & 7) * 2 + core

    def block_owner(to):
        return place(2 * to + zh, y, core)

    def rim_owner(away):
        other = wrapped(chip + away, CHIPS)
        return place(other >> 3, other & 7, core)

    loads = [
        pltpu.make_async_copy(src, dst, load.at[i])
        for i, (src, dst) in enumerate(
            (
                (target_ref, target),
                (column_ref, column),
                (count_ref, count),
                (coef_ref, coef),
                (vec_ref, vec),
                (tiles_ref, tiles),
            )
        )
    ]
    for copy in loads:
        copy.start()
    recv_lab[...] = jnp.zeros(recv_lab.shape, F32)

    barrier = pltpu.get_barrier_semaphore()

    def greet(where):
        @pl.when(jnp.logical_not(is_here(where)))
        def _():
            pl.semaphore_signal(barrier, inc=1, device_id=where, device_id_type=MESH)

    @pl.loop(0, N_ROWS)
    def _(source):
        greet((source, (half & 1) * 16 + at * 2 + core))

    @pl.loop(0, SOURCES)
    def _(p):
        greet(vector_home(p))
        greet(vector_owner(p))

    for away in (-2, 2, -1, 1):
        greet(rim_owner(away))
    greet((row, task + 1 - 2 * core))

    for copy in loads[:-1]:
        copy.wait()
    padded[...] = jnp.zeros(padded.shape, F32)
    padded[:MINE, :] = vec[...].astype(F32)
    mine = padded[...]
    for p in range(SOURCES):
        left = mine[:, p * WIDTH : p * WIDTH + 128]
        right = mine[:, p * WIDTH + 128 : (p + 1) * WIDTH]
        send_v[p] = jnp.concatenate([left, right], axis=0).astype(BF16)

    lane = iota((1, 32), 1)
    second_row = lane >> 4
    first = ((row * N_TASK + task) >> 1) * CHIP_ROWS - OWN * CHIP_ROWS
    live = (lane & 15) < jnp.where(second_row == 1, count[:, 1:2], count[:, 0:1])
    code = jnp.where(live, (column[...] - first) * 2 + second_row + 1, 0)
    send_info[...] = jnp.zeros(send_info.shape, F32)
    send_info[0:1, 0:32] = code.astype(F32)

    targets = target[...]
    diagonal = iota((32, 32), 0) == iota((32, 32), 1)
    as_column = jnp.sum(jnp.where(diagonal, targets, 0).astype(F32), axis=1, keepdims=True)
    as_column = as_column.astype(jnp.int32)
    owner_column, name_column = as_column >> 5, as_column & 31
    owner_row = targets >> 5
    earlier = (owner_column == owner_row) & (iota((32, 32), 1) < iota((32, 32), 0))
    rank = jnp.sum(jnp.where(earlier, 1.0, 0.0), axis=1, keepdims=True)
    slot = (owner_column.astype(F32) * 2.0 + rank) * 8.0
    spread = (iota((32, 256), 1) & 31) == iota((32, 256), 0)
    slots = jnp.sum(jnp.where(spread, slot, 0.0), axis=0, keepdims=True)
    slots = slots.astype(jnp.int32) + (iota((1, 256), 1) >> 5)

    goes_to = one_hot(owner_row == (iota((N_ROWS * 8, 32), 0) >> 3))
    which = ((iota((32, 128), 1) >> 3) & 1).astype(F32) == rank
    named = jnp.where(which, (name_column + 1).astype(F32), 0.0).astype(BF16)
    names = jnp.dot(goes_to, named, preferred_element_type=F32) - 1.0
    send_lab[...] = names.reshape(N_ROWS, 8, 128)

    loads[-1].wait()
    stacked = jnp.concatenate([tiles[:, u * 512 : (u + 1) * 512] for u in range(8)], axis=0)
    packing = one_hot(iota((N_ROWS * 16, 256), 0) == slots)
    packed = jnp.dot(packing, stacked, preferred_element_type=F32)
    send_h[...] = packed.astype(BF16).reshape(N_ROWS, 16, 512)

    block_stays = ((half & 1) == zh) & (at == y)
    vector_stays = (half >> 1) == row
    to_self = jnp.where(block_stays, 1, 0) + 2 * jnp.where(vector_stays, 1, 0)
    pl.semaphore_wait(barrier, N_ROWS + 2 * SOURCES + 5 - to_self)

    slot_v = zh * 8 + y
    one_line = pl.ds(0, 1)
    info_owner = place(2 * row + zh, y, core)

    @pl.loop(0, SOURCES)
    def _(k):
        p = (k & 1) * 8 + ((y + farthest_first(k >> 1, 8)) & 7)
        transfer(send_v.at[p], recv_v.at[slot_v], v_send, v_recv, vector_owner(p))

    transfer(send_info.at[one_line], recv_info.at[one_line], one_send.at[0], info_recv, info_owner)

    @pl.loop(0, N_ROWS)
    def _(k):
        there = wrapped(z + farthest_first(k >> 1, LEVELS), LEVELS)
        to = 2 * there + (k & 1)
        where = block_owner(to)
        transfer(
            send_lab.at[to, one_line], recv_lab.at[row, one_line], lab_send, lab_recv, where
        )
        transfer(send_h.at[to], recv_h.at[row], h_send, h_recv, where)

    def selector(shape, vector_dim, side, source=0):
        where = iota(shape, 1 - vector_dim)
        lane = where & 7
        vector = ((where >> 4) + source) * MINE + lane
        fits = (lane < MINE) & ((where & 8) == 8 * side)
        return one_hot((iota(shape, vector_dim) == vector) & fits)

    def rim(step, part, away):
        rows = pl.ds(part * PART, PART)
        return pltpu.make_async_remote_copy(
            win.at[step, OWN, rows],
            win.at[step, OWN - away, rows],
            rim_send.at[step],
            rim_recv.at[step, part, OWN - away],
            device_id=rim_owner(away),
            device_id_type=MESH,
        )

    def send_rims(step, part):
        for away in (-2, 2, -1, 1):
            rim(step, part, away).start()

    def rims_sent(step):
        arrived(win.at[step, pl.ds(0, 4)], rim_send.at[step])

    def rows_of(part):
        return slice(part * PART, (part + 1) * PART)

    arrived(recv_v, v_recv)
    pieces = recv_v[...].reshape(SOURCES * 16, 128)
    for side in range(2):
        pick = selector((HALF_VECTORS, SOURCES * 16), 0, side)
        got = jnp.dot(pick, pieces, preferred_element_type=F32)
        win[0, OWN, :, side * 128 : (side + 1) * 128] = got.astype(BF16)
    for part in range(GROUPS):
        send_rims(0, part)
    total[...] = coef[:, 0:1] * win[0, OWN].astype(F32)

    arrived(recv_info.at[one_line], info_recv)
    arrived(recv_lab.at[:, one_line], lab_recv)
    wide = (N_ROWS * 8, N_ROWS * 16)
    lab = recv_lab[...].reshape(N_ROWS * 8, 128)
    lab = jnp.concatenate([lab] * 3, axis=1)
    keep = iota(wide, 0) == (iota(wide, 1) >> 4) * 8
    lab = jnp.sum(jnp.where(keep, lab, 0.0), axis=0, keepdims=True)
    on_diagonal = iota((32, 128), 0) == iota((32, 128), 1)
    info = jnp.sum(jnp.where(on_diagonal, recv_info[0:1, :], 0.0), axis=1, keepdims=True)
    at_slot = iota((32, N_ROWS * 16), 0).astype(F32) == lab
    code = jnp.sum(jnp.where(at_slot, info, 0.0), axis=0, keepdims=True) - 1.0
    goes = code * 8.0 + (iota((1, N_ROWS * 16), 1) & 7).astype(F32)
    columns = WINDOW * CHIP_ROWS
    placing = one_hot(iota((columns * 16, N_ROWS * 16), 0).astype(F32) == goes)
    line = iota((128, 128), 0)
    source = (line & 7) * 16 + (line >> 6) * 8 + ((line >> 3) & 7)
    turn = one_hot(iota((128, 128), 1) == source)

    arrived(recv_h, h_recv)
    blocks = recv_h[...].reshape(N_ROWS * 16, 512)
    raw = jnp.dot(placing, blocks, preferred_element_type=F32)
    low = iota((16, 128), 1) < TILE
    for pair_at in range(columns // 2):
        for group in range(4):
            lanes = slice(group * 128, (group + 1) * 128)
            a = raw[pair_at * 32 : pair_at * 32 + 16, lanes]
            b = raw[pair_at * 32 + 16 : pair_at * 32 + 32, lanes]
            even = jnp.where(low, a, pltpu.roll(b, TILE, 1))
            odd = jnp.where(low, pltpu.roll(a, TILE, 1), b)
            to = slice(pair_at * 128, (pair_at + 1) * 128)
            band_raw[group * 32 : group * 32 + 16, to] = even.astype(BF16)
            band_raw[group * 32 + 16 : group * 32 + 32, to] = odd.astype(BF16)
    mine_rows = pl.ds(pl.multiple_of(core * 128, 128), 128)
    band[mine_rows, :] = jnp.dot(turn, band_raw[...], preferred_element_type=F32).astype(BF16)
    sibling = pltpu.make_async_remote_copy(
        band.at[mine_rows],
        band.at[mine_rows],
        one_send.at[1],
        band_recv,
        device_id=(row, task + 1 - 2 * core),
        device_id_type=MESH,
    )
    sibling.start()
    sibling.wait_recv()

    def leave(step):
        if step == 0:
            sent(send_h, h_send, block_stays)
            sent(send_lab.at[:, one_line], lab_send, block_stays)
        elif step == 1:
            sent(send_v, v_send, vector_stays)
            sibling.wait_send()

            @pl.when(jnp.logical_not(block_stays & vector_stays))
            def _():
                arrived(send_info.at[one_line], one_send.at[0])

        if 1 <= step < ITERS:
            rims_sent(step - 1)

    slot_f = (half & 1) * 8 + at
    for step in range(ITERS):
        for part in range(GROUPS):
            rows = rows_of(part)
            product = None
            for j in (OWN, 1, 3, 0, 4):
                if j != OWN:
                    rim(step, part, OWN - j).wait_recv()
                term = lax.dot_general(
                    win[step, j, rows],
                    band[:, j * WIDTH : (j + 1) * WIDTH],
                    (((1,), (1,)), ((), ())),
                    preferred_element_type=F32,
                )
                product = term if product is None else product + term
            if step:
                product = 2.0 * product - win[step - 1, OWN, rows].astype(F32)
            current = product.astype(BF16)
            if step < ITERS - 1:
                win[step + 1, OWN, rows] = current
                send_rims(step + 1, part)
                total[rows] += coef[:, step + 1 : step + 2] * current.astype(F32)
                if part == GROUPS - 1:
                    leave(step)
                continue
            result = total[rows] + coef[:, step + 1 : step + 2] * current.astype(F32)
            results[rows, :] = result.astype(BF16)
            begin, end = part * PART // MINE, (part + 1) * PART // MINE
            spread = None
            for side in range(2):
                put = selector(((end - begin) * 16, (part + 1) * PART), 1, side, begin)
                ready = results[: (part + 1) * PART, side * 128 : (side + 1) * 128]
                term = jnp.dot(put, ready, preferred_element_type=F32)
                spread = term if spread is None else spread + term
            send_f[begin:end] = spread.astype(BF16).reshape(end - begin, 16, 128)

            @pl.loop(begin, end)
            def _(q):
                where = vector_home(q)
                transfer(send_f.at[q], recv_f.at[slot_f], f_send, f_recv, where)

    leave(ITERS - 1)
    rims_sent(ITERS - 1)
    sent(send_f, f_send, vector_stays)
    arrived(recv_f, f_recv)
    final = recv_f[...].astype(F32)
    flat = [final[p, 8 * s : 8 * s + 8, :] for p in range(SOURCES) for s in range(2)]
    out_ref[...] = jnp.concatenate(flat, axis=1).astype(BF16)[:MINE, :]


def local(hamiltonian_tiles, tile_target, column_block, row_count, vectors, expansion_coef):
    dma = pltpu.SemaphoreType.DMA
    vmem = pl.BlockSpec(memory_space=pltpu.VMEM)
    anywhere = pl.BlockSpec(memory_space=pl.ANY)
    return pl.pallas_call(
        kernel,
        out_shape=jax.ShapeDtypeStruct(vectors.shape, BF16),
        in_specs=[anywhere] * 6,
        out_specs=vmem,
        scratch_shapes=[
            pltpu.VMEM((32, TILE * TILE), BF16),
            pltpu.VMEM((1, 32), jnp.int32),
            pltpu.VMEM((1, 32), jnp.int32),
            pltpu.VMEM((1, 2), jnp.int32),
            pltpu.VMEM(vectors.shape, BF16),
            pltpu.VMEM((1, ITERS + 1), F32),
            pltpu.VMEM((PAD, vectors.shape[1]), F32),
            pltpu.VMEM((N_ROWS, 16, 512), BF16),
            pltpu.VMEM((N_ROWS, 16, 512), BF16),
            pltpu.VMEM((N_ROWS, 8, 128), F32),
            pltpu.VMEM((N_ROWS, 8, 128), F32),
            pltpu.VMEM((8, 128), F32),
            pltpu.VMEM((8, 128), F32),
            pltpu.VMEM((SOURCES, 16, 128), BF16),
            pltpu.VMEM((SOURCES, 16, 128), BF16),
            pltpu.VMEM((128, WINDOW * WIDTH), BF16),
            pltpu.VMEM((WIDTH, WINDOW * WIDTH), BF16),
            pltpu.VMEM((ITERS, WINDOW, HALF_VECTORS, WIDTH), BF16),
            pltpu.VMEM((HALF_VECTORS, WIDTH), F32),
            pltpu.VMEM((HALF_VECTORS, WIDTH), BF16),
            pltpu.VMEM((SOURCES, 16, 128), BF16),
            pltpu.VMEM((SOURCES, 16, 128), BF16),
            dma(()),
            dma(()),
            dma(()),
            dma((2,)),
            dma((ITERS,)),
            dma(()),
            dma((6,)),
            dma(()),
            dma(()),
            dma(()),
            dma(()),
            dma(()),
            dma((ITERS, GROUPS, WINDOW)),
            dma(()),
        ],
        compiler_params=pltpu.CompilerParams(
            collective_id=0, has_side_effects=True, vmem_limit_bytes=55104 * 1024
        ),
    )(
        hamiltonian_tiles,
        tile_target[None, :],
        column_block[None, :],
        row_count[None, :],
        vectors,
        expansion_coef[None, :],
    )


def solution(mesh):
    in_specs = (
        P(("rows", "task"), None),
        P(("rows", "task")),
        P(("rows", "task")),
        P(("rows", "task")),
        P("task", "rows"),
        P(),
    )
    out_specs = P("task", "rows")
    return jax.shard_map(local, mesh=mesh, in_specs=in_specs, out_specs=out_specs, check_vma=False)
```

```python
import jax
import jax.numpy as jnp
from jax import lax
from jax.experimental import pallas as pl
from jax.experimental.pallas import tpu as pltpu
from jax.sharding import PartitionSpec as P

TILE = 64
SLOTS_ROW = 16
REACH = 8
ITERS = 4
MESH = pl.DeviceIdType.MESH
F32 = jnp.float32
BF16 = jnp.bfloat16

N_ROWS = 24
N_TASK = 32
CHIPS = 384
LEVELS = 12
CHIP_ROWS = 4
WINDOW = 5
OWN = 2
MINE = 6
PAD = 8
SOURCES = 16
HALF_VECTORS = MINE * SOURCES
GROUPS = 6
PART = HALF_VECTORS // GROUPS
WIDTH = CHIP_ROWS * TILE


def turned(x, z):
    return x + (z & 1) * (3 - 2 * x)


def farthest_first(k, size):
    return (size // 2 - ((k + 1) >> 1)) * (2 * (k & 1) - 1)


def along(at, half):
    return at + (half & 1) * (7 - 2 * at)


def place(half, at, core):
    z = half >> 2
    x = turned(half & 3, z)
    upper = jnp.where(z >= 6, 1, 0)
    return (z - 6 * upper) * 4 + x, upper * 16 + along(at, half) * 2 + core


def wrapped(index, size):
    index = jnp.where(index >= size, index - size, index)
    return jnp.where(index < 0, index + size, index)


def one_hot(condition):
    return jnp.where(condition, 1.0, 0.0).astype(BF16)


def iota(shape, dim):
    return lax.broadcasted_iota(jnp.int32, shape, dim)


def kernel(
    tiles_ref, target_ref, column_ref, count_ref, vec_ref, coef_ref, out_ref,
    tiles, target, column, count, vec, coef, padded, send_h, recv_h, send_lab, recv_lab, send_info, recv_info, send_v, recv_v,
    band_raw, band, band_t, win, total, results, send_f, recv_f,
    h_send, lab_send, v_send, one_send, rim_send, f_send,
    load, h_recv, lab_recv, v_recv, info_recv, band_recv, rim_recv, f_recv,
):
    row, task = lax.axis_index("rows"), lax.axis_index("task")
    zh, y, core = task >> 4, (task >> 1) & 7, task & 1
    z, x = zh * 6 + (row >> 2), row & 3
    half = 4 * z + turned(x, z)
    at = along(y, half)
    chip = half * 8 + at

    def is_here(where):
        return (where[0] == row) & (where[1] == task)

    def send(src, dst, send_sem, recv_sem, where):
        pltpu.make_async_remote_copy(
            src, dst, send_sem, recv_sem, device_id=where, device_id_type=MESH
        ).start()

    def transfer(src, dst, send_sem, recv_sem, where):
        here = is_here(where)

        @pl.when(here)
        def _():
            pltpu.make_async_copy(src, dst, recv_sem).start()

        @pl.when(jnp.logical_not(here))
        def _():
            send(src, dst, send_sem, recv_sem, where)

    def arrived(buffer, sem):
        pltpu.make_async_copy(buffer, buffer, sem).wait()

    def sent(buffer, sem, one_stays):
        @pl.when(one_stays)
        def _():
            arrived(buffer.at[pl.ds(1, buffer.shape[0] - 1)], sem)

        @pl.when(jnp.logical_not(one_stays))
        def _():
            arrived(buffer, sem)

    def vector_owner(p):
        return place(2 * row + (p >> 3), p & 7, core)

    def vector_home(q):
        return half >> 1, (q >> 3) * 16 + (q & 7) * 2 + core

    def block_owner(to):
        return place(2 * to + zh, y, core)

    def rim_owner(away):
        other = wrapped(chip + away, CHIPS)
        return place(other >> 3, other & 7, core)

    loads = [
        pltpu.make_async_copy(src, dst, load.at[i])
        for i, (src, dst) in enumerate(
            (
                (target_ref, target),
                (column_ref, column),
                (count_ref, count),
                (coef_ref, coef),
                (vec_ref, vec),
                (tiles_ref, tiles),
            )
        )
    ]
    for copy in loads:
        copy.start()
    recv_lab[...] = jnp.zeros(recv_lab.shape, F32)

    barrier = pltpu.get_barrier_semaphore()

    def greet(where):
        pl.semaphore_signal(barrier, inc=1, device_id=where, device_id_type=MESH)

    block_stays = ((half & 1) == zh) & (at == y)
    vector_stays = (half >> 1) == row
    slot_v, slot_f = zh * 8 + y, (half & 1) * 8 + at

    def block_home(source):
        return source, (half & 1) * 16 + at * 2 + core

    @pl.loop(1, N_ROWS)
    def _(k):
        greet(block_home(wrapped(row + k, N_ROWS)))

    @pl.loop(1, SOURCES)
    def _(k):
        greet(vector_home((slot_v + k) & 15))
        greet(vector_owner((slot_f + k) & 15))

    @pl.when(jnp.logical_not(block_stays))
    def _():
        greet(block_home(row))

    @pl.when(jnp.logical_not(vector_stays))
    def _():
        greet(vector_home(slot_v))
        greet(vector_owner(slot_f))

    for away in (-2, 2, -1, 1):
        greet(rim_owner(away))
    greet((row, task + 1 - 2 * core))

    for copy in loads[:-1]:
        copy.wait()
    padded[...] = jnp.zeros(padded.shape, F32)
    padded[:MINE, :] = vec[...].astype(F32)
    mine = padded[...]
    for p in range(SOURCES):
        left = mine[:, p * WIDTH : p * WIDTH + 128]
        right = mine[:, p * WIDTH + 128 : (p + 1) * WIDTH]
        send_v[p] = jnp.concatenate([left, right], axis=0).astype(BF16)

    lane = iota((1, 32), 1)
    second_row = lane >> 4
    first = ((row * N_TASK + task) >> 1) * CHIP_ROWS - OWN * CHIP_ROWS
    live = (lane & 15) < jnp.where(second_row == 1, count[:, 1:2], count[:, 0:1])
    code = jnp.where(live, (column[...] - first) * 2 + second_row + 1, 0)
    send_info[...] = jnp.zeros(send_info.shape, F32)
    send_info[0:1, 0:32] = code.astype(F32)

    targets = target[...]
    diagonal = iota((32, 32), 0) == iota((32, 32), 1)
    as_column = jnp.sum(jnp.where(diagonal, targets, 0).astype(F32), axis=1, keepdims=True)
    as_column = as_column.astype(jnp.int32)
    owner_column, name_column = as_column >> 5, as_column & 31
    owner_row = targets >> 5
    earlier = (owner_column == owner_row) & (iota((32, 32), 1) < iota((32, 32), 0))
    rank = jnp.sum(jnp.where(earlier, 1.0, 0.0), axis=1, keepdims=True)
    slot = (owner_column.astype(F32) * 2.0 + rank) * 8.0
    spread = (iota((32, 256), 1) & 31) == iota((32, 256), 0)
    slots = jnp.sum(jnp.where(spread, slot, 0.0), axis=0, keepdims=True)
    slots = slots.astype(jnp.int32) + (iota((1, 256), 1) >> 5)

    goes_to = one_hot(owner_row == (iota((N_ROWS * 8, 32), 0) >> 3))
    which = ((iota((32, 128), 1) >> 3) & 1).astype(F32) == rank
    named = jnp.where(which, (name_column + 1).astype(F32), 0.0).astype(BF16)
    names = jnp.dot(goes_to, named, preferred_element_type=F32) - 1.0
    send_lab[...] = names.reshape(N_ROWS, 8, 128)

    loads[-1].wait()
    stacked = jnp.concatenate([tiles[:, u * 512 : (u + 1) * 512] for u in range(8)], axis=0)
    packing = one_hot(iota((N_ROWS * 16, 256), 0) == slots)
    packed = jnp.dot(packing, stacked, preferred_element_type=F32)
    send_h[...] = packed.astype(BF16).reshape(N_ROWS, 16, 512)

    to_self = jnp.where(block_stays, 1, 0) + 2 * jnp.where(vector_stays, 1, 0)
    pl.semaphore_wait(barrier, N_ROWS + 2 * SOURCES + 5 - to_self)

    one_line = pl.ds(0, 1)
    info_owner = place(2 * row + zh, y, core)

    def send_vectors(k, move):
        p = (slot_f + k) & 15
        move(send_v.at[p], recv_v.at[slot_v], v_send, v_recv, vector_owner(p))

    @pl.loop(1, SOURCES)
    def _(k):
        send_vectors(k, send)

    send_vectors(0, transfer)

    transfer(send_info.at[one_line], recv_info.at[one_line], one_send.at[0], info_recv, info_owner)

    def send_blocks(k, move):
        there = wrapped(z + farthest_first(k >> 1, LEVELS), LEVELS)
        to = 2 * there + (k & 1)
        where = block_owner(to)
        lab = send_lab.at[to, one_line], recv_lab.at[row, one_line]
        move(*lab, lab_send, lab_recv, where)
        move(send_h.at[to], recv_h.at[row], h_send, h_recv, where)

    @pl.loop(0, N_ROWS - 2)
    def _(k):
        send_blocks(k, send)

    for k in (N_ROWS - 2, N_ROWS - 1):
        send_blocks(k, transfer)

    def selector(shape, vector_dim, side, source=0):
        where = iota(shape, 1 - vector_dim)
        lane = where & 7
        vector = ((where >> 4) + source) * MINE + lane
        fits = (lane < MINE) & ((where & 8) == 8 * side)
        return one_hot((iota(shape, vector_dim) == vector) & fits)

    def rim(step, part, away):
        rows = pl.ds(part * PART, PART)
        return pltpu.make_async_remote_copy(
            win.at[step, OWN, rows],
            win.at[step, OWN - away, rows],
            rim_send.at[step],
            rim_recv.at[step, part, OWN - away],
            device_id=rim_owner(away),
            device_id_type=MESH,
        )

    def send_rims(step, part):
        for away in (-2, 2, -1, 1):
            rim(step, part, away).start()

    def rims_sent(step):
        arrived(win.at[step, pl.ds(0, 4)], rim_send.at[step])

    def rows_of(part):
        return slice(part * PART, (part + 1) * PART)

    arrived(recv_v, v_recv)
    pieces = recv_v[...].reshape(SOURCES * 16, 128)
    for side in range(2):
        pick = selector((HALF_VECTORS, SOURCES * 16), 0, side)
        got = jnp.dot(pick, pieces, preferred_element_type=F32)
        win[0, OWN, :, side * 128 : (side + 1) * 128] = got.astype(BF16)
    for part in range(GROUPS):
        send_rims(0, part)
    total[...] = coef[:, 0:1] * win[0, OWN].astype(F32)

    arrived(recv_info.at[one_line], info_recv)
    arrived(recv_lab.at[:, one_line], lab_recv)
    wide = (N_ROWS * 8, N_ROWS * 16)
    lab = recv_lab[...].reshape(N_ROWS * 8, 128)
    lab = jnp.concatenate([lab] * 3, axis=1)
    keep = iota(wide, 0) == (iota(wide, 1) >> 4) * 8
    lab = jnp.sum(jnp.where(keep, lab, 0.0), axis=0, keepdims=True)
    on_diagonal = iota((32, 128), 0) == iota((32, 128), 1)
    info = jnp.sum(jnp.where(on_diagonal, recv_info[0:1, :], 0.0), axis=1, keepdims=True)
    at_slot = iota((32, N_ROWS * 16), 0).astype(F32) == lab
    code = jnp.sum(jnp.where(at_slot, info, 0.0), axis=0, keepdims=True) - 1.0
    goes = code * 8.0 + (iota((1, N_ROWS * 16), 1) & 7).astype(F32)
    columns = WINDOW * CHIP_ROWS
    placing = one_hot(iota((columns * 16, N_ROWS * 16), 0).astype(F32) == goes)
    line = iota((128, 128), 0)
    source = (line & 7) * 16 + (line >> 6) * 8 + ((line >> 3) & 7)
    turn = one_hot(iota((128, 128), 1) == source)

    arrived(recv_h, h_recv)
    blocks = recv_h[...].reshape(N_ROWS * 16, 512)
    raw = jnp.dot(placing, blocks, preferred_element_type=F32)
    low = iota((16, 128), 1) < TILE
    for pair_at in range(columns // 2):
        for group in range(4):
            lanes = slice(group * 128, (group + 1) * 128)
            a = raw[pair_at * 32 : pair_at * 32 + 16, lanes]
            b = raw[pair_at * 32 + 16 : pair_at * 32 + 32, lanes]
            even = jnp.where(low, a, pltpu.roll(b, TILE, 1))
            odd = jnp.where(low, pltpu.roll(a, TILE, 1), b)
            to = slice(pair_at * 128, (pair_at + 1) * 128)
            band_raw[group * 32 : group * 32 + 16, to] = even.astype(BF16)
            band_raw[group * 32 + 16 : group * 32 + 32, to] = odd.astype(BF16)
    mine_rows = pl.ds(pl.multiple_of(core * 128, 128), 128)
    band[mine_rows, :] = jnp.dot(turn, band_raw[...], preferred_element_type=F32).astype(BF16)
    sibling = pltpu.make_async_remote_copy(
        band.at[mine_rows],
        band.at[mine_rows],
        one_send.at[1],
        band_recv,
        device_id=(row, task + 1 - 2 * core),
        device_id_type=MESH,
    )
    sibling.start()
    sibling.wait_recv()
    band_t[...] = band[...].T

    def leave(step):
        if step == 0:
            sent(send_h, h_send, block_stays)
            sent(send_lab.at[:, one_line], lab_send, block_stays)
        elif step == 1:
            sent(send_v, v_send, vector_stays)
            sibling.wait_send()

            @pl.when(jnp.logical_not(block_stays & vector_stays))
            def _():
                arrived(send_info.at[one_line], one_send.at[0])

        if 1 <= step < ITERS:
            rims_sent(step - 1)

    for step in range(ITERS):
        for part in range(GROUPS):
            rows = rows_of(part)
            product = None
            for j in (OWN, 1, 3, 0, 4):
                if j != OWN:
                    rim(step, part, OWN - j).wait_recv()
                term = lax.dot_general(
                    win[step, j, rows],
                    band_t[j * WIDTH : (j + 1) * WIDTH, :],
                    (((1,), (0,)), ((), ())),
                    preferred_element_type=F32,
                )
                product = term if product is None else product + term
            if step:
                product = 2.0 * product - win[step - 1, OWN, rows].astype(F32)
            current = product.astype(BF16)
            if step < ITERS - 1:
                win[step + 1, OWN, rows] = current
                send_rims(step + 1, part)
                total[rows] += coef[:, step + 1 : step + 2] * current.astype(F32)
                if part == GROUPS - 1:
                    leave(step)
                continue
            result = total[rows] + coef[:, step + 1 : step + 2] * current.astype(F32)
            results[rows, :] = result.astype(BF16)
            begin, end = part * PART // MINE, (part + 1) * PART // MINE
            spread = None
            for side in range(2):
                put = selector(((end - begin) * 16, (part + 1) * PART), 1, side, begin)
                ready = results[: (part + 1) * PART, side * 128 : (side + 1) * 128]
                term = jnp.dot(put, ready, preferred_element_type=F32)
                spread = term if spread is None else spread + term
            send_f[begin:end] = spread.astype(BF16).reshape(end - begin, 16, 128)

            @pl.loop(begin, end)
            def _(q):
                where = vector_home(q)
                transfer(send_f.at[q], recv_f.at[slot_f], f_send, f_recv, where)

    leave(ITERS - 1)
    rims_sent(ITERS - 1)
    sent(send_f, f_send, vector_stays)
    arrived(recv_f, f_recv)
    final = recv_f[...].astype(F32)
    flat = [final[p, 8 * s : 8 * s + 8, :] for p in range(SOURCES) for s in range(2)]
    out_ref[...] = jnp.concatenate(flat, axis=1).astype(BF16)[:MINE, :]


def local(hamiltonian_tiles, tile_target, column_block, row_count, vectors, expansion_coef):
    dma = pltpu.SemaphoreType.DMA
    vmem = pl.BlockSpec(memory_space=pltpu.VMEM)
    anywhere = pl.BlockSpec(memory_space=pl.ANY)
    return pl.pallas_call(
        kernel,
        out_shape=jax.ShapeDtypeStruct(vectors.shape, BF16),
        in_specs=[anywhere] * 6,
        out_specs=vmem,
        scratch_shapes=[
            pltpu.VMEM((32, TILE * TILE), BF16),
            pltpu.VMEM((1, 32), jnp.int32),
            pltpu.VMEM((1, 32), jnp.int32),
            pltpu.VMEM((1, 2), jnp.int32),
            pltpu.VMEM(vectors.shape, BF16),
            pltpu.VMEM((1, ITERS + 1), F32),
            pltpu.VMEM((PAD, vectors.shape[1]), F32),
            pltpu.VMEM((N_ROWS, 16, 512), BF16),
            pltpu.VMEM((N_ROWS, 16, 512), BF16),
            pltpu.VMEM((N_ROWS, 8, 128), F32),
            pltpu.VMEM((N_ROWS, 8, 128), F32),
            pltpu.VMEM((8, 128), F32),
            pltpu.VMEM((8, 128), F32),
            pltpu.VMEM((SOURCES, 16, 128), BF16),
            pltpu.VMEM((SOURCES, 16, 128), BF16),
            pltpu.VMEM((128, WINDOW * WIDTH), BF16),
            pltpu.VMEM((WIDTH, WINDOW * WIDTH), BF16),
            pltpu.VMEM((WINDOW * WIDTH, WIDTH), BF16),
            pltpu.VMEM((ITERS, WINDOW, HALF_VECTORS, WIDTH), BF16),
            pltpu.VMEM((HALF_VECTORS, WIDTH), F32),
            pltpu.VMEM((HALF_VECTORS, WIDTH), BF16),
            pltpu.VMEM((SOURCES, 16, 128), BF16),
            pltpu.VMEM((SOURCES, 16, 128), BF16),
            dma(()),
            dma(()),
            dma(()),
            dma((2,)),
            dma((ITERS,)),
            dma(()),
            dma((6,)),
            dma(()),
            dma(()),
            dma(()),
            dma(()),
            dma(()),
            dma((ITERS, GROUPS, WINDOW)),
            dma(()),
        ],
        compiler_params=pltpu.CompilerParams(
            collective_id=0, has_side_effects=True, vmem_limit_bytes=55104 * 1024
        ),
    )(
        hamiltonian_tiles,
        tile_target[None, :],
        column_block[None, :],
        row_count[None, :],
        vectors,
        expansion_coef[None, :],
    )


def solution(mesh):
    in_specs = (
        P(("rows", "task"), None),
        P(("rows", "task")),
        P(("rows", "task")),
        P(("rows", "task")),
        P("task", "rows"),
        P(),
    )
    out_specs = P("task", "rows")
    return jax.shard_map(local, mesh=mesh, in_specs=in_specs, out_specs=out_specs, check_vma=False)
```

```python
import jax
import jax.numpy as jnp
from jax import lax
from jax.experimental import pallas as pl
from jax.experimental.pallas import tpu as pltpu
from jax.sharding import PartitionSpec as P

TILE = 64
SLOTS_ROW = 16
REACH = 8
ITERS = 4
MESH = pl.DeviceIdType.MESH
F32 = jnp.float32
BF16 = jnp.bfloat16

N_ROWS = 24
N_TASK = 32
CHIPS = 384
LEVELS = 12
CHIP_ROWS = 4
WINDOW = 5
OWN = 2
MINE = 6
PAD = 8
SOURCES = 16
HALF_VECTORS = MINE * SOURCES
GROUPS = 6
PART = HALF_VECTORS // GROUPS
WIDTH = CHIP_ROWS * TILE
HALF_BAND = WINDOW * WIDTH // 2


def turned(x, z):
    return x + (z & 1) * (3 - 2 * x)


def farthest_first(k, size):
    return (size // 2 - ((k + 1) >> 1)) * (2 * (k & 1) - 1)


def along(at, half):
    return at + (half & 1) * (7 - 2 * at)


def place(half, at, core):
    z = half >> 2
    x = turned(half & 3, z)
    upper = jnp.where(z >= 6, 1, 0)
    return (z - 6 * upper) * 4 + x, upper * 16 + along(at, half) * 2 + core


def wrapped(index, size):
    index = jnp.where(index >= size, index - size, index)
    return jnp.where(index < 0, index + size, index)


def one_hot(condition):
    return jnp.where(condition, 1.0, 0.0).astype(BF16)


def iota(shape, dim):
    return lax.broadcasted_iota(jnp.int32, shape, dim)


def kernel(
    tiles_ref, target_ref, column_ref, count_ref, vec_ref, coef_ref, out_ref,
    tiles, target, column, count, vec, coef, padded, send_h, recv_h, send_lab, recv_lab, send_info, recv_info, send_v, recv_v,
    band_raw, band, band_t, win, total, results, send_f, recv_f,
    h_send, lab_send, v_send, one_send, rim_send, f_send,
    load, h_recv, lab_recv, v_recv, info_recv, band_recv, rim_recv, f_recv,
):
    row, task = lax.axis_index("rows"), lax.axis_index("task")
    zh, y, core = task >> 4, (task >> 1) & 7, task & 1
    z, x = zh * 6 + (row >> 2), row & 3
    half = 4 * z + turned(x, z)
    at = along(y, half)
    chip = half * 8 + at

    def is_here(where):
        return (where[0] == row) & (where[1] == task)

    def send(src, dst, send_sem, recv_sem, where):
        pltpu.make_async_remote_copy(
            src, dst, send_sem, recv_sem, device_id=where, device_id_type=MESH
        ).start()

    def transfer(src, dst, send_sem, recv_sem, where):
        here = is_here(where)

        @pl.when(here)
        def _():
            pltpu.make_async_copy(src, dst, recv_sem).start()

        @pl.when(jnp.logical_not(here))
        def _():
            send(src, dst, send_sem, recv_sem, where)

    def arrived(buffer, sem):
        pltpu.make_async_copy(buffer, buffer, sem).wait()

    def sent(buffer, sem, one_stays):
        @pl.when(one_stays)
        def _():
            arrived(buffer.at[pl.ds(1, buffer.shape[0] - 1)], sem)

        @pl.when(jnp.logical_not(one_stays))
        def _():
            arrived(buffer, sem)

    def vector_owner(p):
        return place(2 * row + (p >> 3), p & 7, core)

    def vector_home(q):
        return half >> 1, (q >> 3) * 16 + (q & 7) * 2 + core

    def block_owner(to):
        return place(2 * to + zh, y, core)

    def rim_owner(away):
        other = wrapped(chip + away, CHIPS)
        return place(other >> 3, other & 7, core)

    loads = [
        pltpu.make_async_copy(src, dst, load.at[i])
        for i, (src, dst) in enumerate(
            (
                (target_ref, target),
                (column_ref, column),
                (count_ref, count),
                (coef_ref, coef),
                (vec_ref, vec),
                (tiles_ref, tiles),
            )
        )
    ]
    for copy in loads:
        copy.start()
    recv_lab[...] = jnp.zeros(recv_lab.shape, F32)

    barrier = pltpu.get_barrier_semaphore()

    def greet(where):
        pl.semaphore_signal(barrier, inc=1, device_id=where, device_id_type=MESH)

    block_stays = ((half & 1) == zh) & (at == y)
    vector_stays = (half >> 1) == row
    slot_v, slot_f = zh * 8 + y, (half & 1) * 8 + at

    def block_home(source):
        return source, (half & 1) * 16 + at * 2 + core

    @pl.loop(1, N_ROWS)
    def _(k):
        greet(block_home(wrapped(row + k, N_ROWS)))

    @pl.loop(1, SOURCES)
    def _(k):
        greet(vector_home((slot_v + k) & 15))
        greet(vector_owner((slot_f + k) & 15))

    @pl.when(jnp.logical_not(block_stays))
    def _():
        greet(block_home(row))

    @pl.when(jnp.logical_not(vector_stays))
    def _():
        greet(vector_home(slot_v))
        greet(vector_owner(slot_f))

    for away in (-2, 2, -1, 1):
        greet(rim_owner(away))
    greet((row, task + 1 - 2 * core))

    for copy in loads[:-1]:
        copy.wait()
    padded[...] = jnp.zeros(padded.shape, F32)
    padded[:MINE, :] = vec[...].astype(F32)
    mine = padded[...]
    for p in range(SOURCES):
        left = mine[:, p * WIDTH : p * WIDTH + 128]
        right = mine[:, p * WIDTH + 128 : (p + 1) * WIDTH]
        send_v[p] = jnp.concatenate([left, right], axis=0).astype(BF16)

    lane = iota((1, 32), 1)
    second_row = lane >> 4
    first = ((row * N_TASK + task) >> 1) * CHIP_ROWS - OWN * CHIP_ROWS
    live = (lane & 15) < jnp.where(second_row == 1, count[:, 1:2], count[:, 0:1])
    code = jnp.where(live, (column[...] - first) * 2 + second_row + 1, 0)
    send_info[...] = jnp.zeros(send_info.shape, F32)
    send_info[0:1, 0:32] = code.astype(F32)

    targets = target[...]
    diagonal = iota((32, 32), 0) == iota((32, 32), 1)
    as_column = jnp.sum(jnp.where(diagonal, targets, 0).astype(F32), axis=1, keepdims=True)
    as_column = as_column.astype(jnp.int32)
    owner_column, name_column = as_column >> 5, as_column & 31
    owner_row = targets >> 5
    earlier = (owner_column == owner_row) & (iota((32, 32), 1) < iota((32, 32), 0))
    rank = jnp.sum(jnp.where(earlier, 1.0, 0.0), axis=1, keepdims=True)
    slot = (owner_column.astype(F32) * 2.0 + rank) * 8.0
    spread = (iota((32, 256), 1) & 31) == iota((32, 256), 0)
    slots = jnp.sum(jnp.where(spread, slot, 0.0), axis=0, keepdims=True)
    slots = slots.astype(jnp.int32) + (iota((1, 256), 1) >> 5)

    goes_to = one_hot(owner_row == (iota((N_ROWS * 8, 32), 0) >> 3))
    which = ((iota((32, 128), 1) >> 3) & 1).astype(F32) == rank
    named = jnp.where(which, (name_column + 1).astype(F32), 0.0).astype(BF16)
    names = jnp.dot(goes_to, named, preferred_element_type=F32) - 1.0
    send_lab[...] = names.reshape(N_ROWS, 8, 128)

    loads[-1].wait()
    stacked = jnp.concatenate([tiles[:, u * 512 : (u + 1) * 512] for u in range(8)], axis=0)
    packing = one_hot(iota((N_ROWS * 16, 256), 0) == slots)
    packed = jnp.dot(packing, stacked, preferred_element_type=F32)
    send_h[...] = packed.astype(BF16).reshape(N_ROWS, 16, 512)

    to_self = jnp.where(block_stays, 1, 0) + 2 * jnp.where(vector_stays, 1, 0)
    pl.semaphore_wait(barrier, N_ROWS + 2 * SOURCES + 5 - to_self)

    one_line = pl.ds(0, 1)
    info_owner = place(2 * row + zh, y, core)

    def send_vectors(k, move):
        p = (slot_f + k) & 15
        move(send_v.at[p], recv_v.at[slot_v], v_send, v_recv, vector_owner(p))

    @pl.loop(1, SOURCES)
    def _(k):
        send_vectors(k, send)

    send_vectors(0, transfer)

    transfer(send_info.at[one_line], recv_info.at[one_line], one_send.at[0], info_recv, info_owner)

    def send_blocks(k, move):
        there = wrapped(z + farthest_first(k >> 1, LEVELS), LEVELS)
        to = 2 * there + (k & 1)
        where = block_owner(to)
        lab = send_lab.at[to, one_line], recv_lab.at[row, one_line]
        move(*lab, lab_send, lab_recv, where)
        move(send_h.at[to], recv_h.at[row], h_send, h_recv, where)

    @pl.loop(0, N_ROWS - 2)
    def _(k):
        send_blocks(k, send)

    for k in (N_ROWS - 2, N_ROWS - 1):
        send_blocks(k, transfer)

    def selector(shape, vector_dim, side, source=0):
        where = iota(shape, 1 - vector_dim)
        lane = where & 7
        vector = ((where >> 4) + source) * MINE + lane
        fits = (lane < MINE) & ((where & 8) == 8 * side)
        return one_hot((iota(shape, vector_dim) == vector) & fits)

    def rim(step, part, away):
        rows = pl.ds(part * PART, PART)
        return pltpu.make_async_remote_copy(
            win.at[step, OWN, rows],
            win.at[step, OWN - away, rows],
            rim_send.at[step],
            rim_recv.at[step, part, OWN - away],
            device_id=rim_owner(away),
            device_id_type=MESH,
        )

    def send_rims(step, part):
        for away in (-2, 2, -1, 1):
            rim(step, part, away).start()

    def rims_sent(step):
        arrived(win.at[step, pl.ds(0, 4)], rim_send.at[step])

    def rows_of(part):
        return slice(part * PART, (part + 1) * PART)

    arrived(recv_v, v_recv)
    pieces = recv_v[...].reshape(SOURCES * 16, 128)
    for side in range(2):
        pick = selector((HALF_VECTORS, SOURCES * 16), 0, side)
        got = jnp.dot(pick, pieces, preferred_element_type=F32)
        win[0, OWN, :, side * 128 : (side + 1) * 128] = got.astype(BF16)
    for part in range(GROUPS):
        send_rims(0, part)
    total[...] = coef[:, 0:1] * win[0, OWN].astype(F32)

    arrived(recv_info.at[one_line], info_recv)
    arrived(recv_lab.at[:, one_line], lab_recv)
    wide = (N_ROWS * 8, N_ROWS * 16)
    lab = recv_lab[...].reshape(N_ROWS * 8, 128)
    lab = jnp.concatenate([lab] * 3, axis=1)
    keep = iota(wide, 0) == (iota(wide, 1) >> 4) * 8
    lab = jnp.sum(jnp.where(keep, lab, 0.0), axis=0, keepdims=True)
    on_diagonal = iota((32, 128), 0) == iota((32, 128), 1)
    info = jnp.sum(jnp.where(on_diagonal, recv_info[0:1, :], 0.0), axis=1, keepdims=True)
    at_slot = iota((32, N_ROWS * 16), 0).astype(F32) == lab
    code = jnp.sum(jnp.where(at_slot, info, 0.0), axis=0, keepdims=True) - 1.0
    goes = code * 8.0 + (iota((1, N_ROWS * 16), 1) & 7).astype(F32)
    columns = WINDOW * CHIP_ROWS
    placing = one_hot(iota((columns * 16, N_ROWS * 16), 0).astype(F32) == goes)
    line = iota((128, 128), 0)
    source = (line & 7) * 16 + (line >> 6) * 8 + ((line >> 3) & 7)
    turn = one_hot(iota((128, 128), 1) == source)

    arrived(recv_h, h_recv)
    blocks = recv_h[...].reshape(N_ROWS * 16, 512)
    raw = jnp.dot(placing, blocks, preferred_element_type=F32)
    low = iota((16, 128), 1) < TILE
    for pair_at in range(columns // 2):
        for group in range(4):
            lanes = slice(group * 128, (group + 1) * 128)
            a = raw[pair_at * 32 : pair_at * 32 + 16, lanes]
            b = raw[pair_at * 32 + 16 : pair_at * 32 + 32, lanes]
            even = jnp.where(low, a, pltpu.roll(b, TILE, 1))
            odd = jnp.where(low, pltpu.roll(a, TILE, 1), b)
            to = slice(pair_at * 128, (pair_at + 1) * 128)
            band_raw[group * 32 : group * 32 + 16, to] = even.astype(BF16)
            band_raw[group * 32 + 16 : group * 32 + 32, to] = odd.astype(BF16)
    mine_rows = pl.ds(pl.multiple_of(core * 128, 128), 128)
    siblings = []
    for piece in range(2):
        columns = slice(piece * HALF_BAND, (piece + 1) * HALF_BAND)
        turned_rows = jnp.dot(turn, band_raw[:, columns], preferred_element_type=F32)
        band[mine_rows, columns] = turned_rows.astype(BF16)
        copy = pltpu.make_async_remote_copy(
            band.at[mine_rows, columns],
            band.at[mine_rows, columns],
            one_send.at[1 + piece],
            band_recv.at[piece],
            device_id=(row, task + 1 - 2 * core),
            device_id_type=MESH,
        )
        copy.start()
        siblings.append(copy)
    their_rows = pl.ds(pl.multiple_of((1 - core) * 128, 128), 128)
    band_t[:, mine_rows] = band[mine_rows, :].T
    for piece in range(2):
        columns = slice(piece * HALF_BAND, (piece + 1) * HALF_BAND)
        siblings[piece].wait_recv()
        band_t[columns, their_rows] = band[their_rows, columns].T

    def leave(step):
        if step == 0:
            sent(send_h, h_send, block_stays)
            sent(send_lab.at[:, one_line], lab_send, block_stays)
        elif step == 1:
            sent(send_v, v_send, vector_stays)
            for copy in siblings:
                copy.wait_send()

            @pl.when(jnp.logical_not(block_stays & vector_stays))
            def _():
                arrived(send_info.at[one_line], one_send.at[0])

        if 1 <= step < ITERS:
            rims_sent(step - 1)

    for step in range(ITERS):
        for part in range(GROUPS):
            rows = rows_of(part)
            product = None
            for j in (OWN, 1, 3, 0, 4):
                if j != OWN:
                    rim(step, part, OWN - j).wait_recv()
                term = lax.dot_general(
                    win[step, j, rows],
                    band_t[j * WIDTH : (j + 1) * WIDTH, :],
                    (((1,), (0,)), ((), ())),
                    preferred_element_type=F32,
                )
                product = term if product is None else product + term
            if step:
                product = 2.0 * product - win[step - 1, OWN, rows].astype(F32)
            current = product.astype(BF16)
            if step < ITERS - 1:
                win[step + 1, OWN, rows] = current
                send_rims(step + 1, part)
                total[rows] += coef[:, step + 1 : step + 2] * current.astype(F32)
                if part == GROUPS - 1:
                    leave(step)
                continue
            result = total[rows] + coef[:, step + 1 : step + 2] * current.astype(F32)
            results[rows, :] = result.astype(BF16)
            begin, end = part * PART // MINE, (part + 1) * PART // MINE
            spread = None
            for side in range(2):
                put = selector(((end - begin) * 16, (part + 1) * PART), 1, side, begin)
                ready = results[: (part + 1) * PART, side * 128 : (side + 1) * 128]
                term = jnp.dot(put, ready, preferred_element_type=F32)
                spread = term if spread is None else spread + term
            send_f[begin:end] = spread.astype(BF16).reshape(end - begin, 16, 128)

            @pl.loop(begin, end)
            def _(q):
                where = vector_home(q)
                transfer(send_f.at[q], recv_f.at[slot_f], f_send, f_recv, where)

    leave(ITERS - 1)
    rims_sent(ITERS - 1)
    sent(send_f, f_send, vector_stays)
    arrived(recv_f, f_recv)
    final = recv_f[...].astype(F32)
    flat = [final[p, 8 * s : 8 * s + 8, :] for p in range(SOURCES) for s in range(2)]
    out_ref[...] = jnp.concatenate(flat, axis=1).astype(BF16)[:MINE, :]


def local(hamiltonian_tiles, tile_target, column_block, row_count, vectors, expansion_coef):
    dma = pltpu.SemaphoreType.DMA
    vmem = pl.BlockSpec(memory_space=pltpu.VMEM)
    anywhere = pl.BlockSpec(memory_space=pl.ANY)
    return pl.pallas_call(
        kernel,
        out_shape=jax.ShapeDtypeStruct(vectors.shape, BF16),
        in_specs=[anywhere] * 6,
        out_specs=vmem,
        scratch_shapes=[
            pltpu.VMEM((32, TILE * TILE), BF16),
            pltpu.VMEM((1, 32), jnp.int32),
            pltpu.VMEM((1, 32), jnp.int32),
            pltpu.VMEM((1, 2), jnp.int32),
            pltpu.VMEM(vectors.shape, BF16),
            pltpu.VMEM((1, ITERS + 1), F32),
            pltpu.VMEM((PAD, vectors.shape[1]), F32),
            pltpu.VMEM((N_ROWS, 16, 512), BF16),
            pltpu.VMEM((N_ROWS, 16, 512), BF16),
            pltpu.VMEM((N_ROWS, 8, 128), F32),
            pltpu.VMEM((N_ROWS, 8, 128), F32),
            pltpu.VMEM((8, 128), F32),
            pltpu.VMEM((8, 128), F32),
            pltpu.VMEM((SOURCES, 16, 128), BF16),
            pltpu.VMEM((SOURCES, 16, 128), BF16),
            pltpu.VMEM((128, WINDOW * WIDTH), BF16),
            pltpu.VMEM((WIDTH, WINDOW * WIDTH), BF16),
            pltpu.VMEM((WINDOW * WIDTH, WIDTH), BF16),
            pltpu.VMEM((ITERS, WINDOW, HALF_VECTORS, WIDTH), BF16),
            pltpu.VMEM((HALF_VECTORS, WIDTH), F32),
            pltpu.VMEM((HALF_VECTORS, WIDTH), BF16),
            pltpu.VMEM((SOURCES, 16, 128), BF16),
            pltpu.VMEM((SOURCES, 16, 128), BF16),
            dma(()),
            dma(()),
            dma(()),
            dma((3,)),
            dma((ITERS,)),
            dma(()),
            dma((6,)),
            dma(()),
            dma(()),
            dma(()),
            dma(()),
            dma((2,)),
            dma((ITERS, GROUPS, WINDOW)),
            dma(()),
        ],
        compiler_params=pltpu.CompilerParams(
            collective_id=0, has_side_effects=True, vmem_limit_bytes=55104 * 1024
        ),
    )(
        hamiltonian_tiles,
        tile_target[None, :],
        column_block[None, :],
        row_count[None, :],
        vectors,
        expansion_coef[None, :],
    )


def solution(mesh):
    in_specs = (
        P(("rows", "task"), None),
        P(("rows", "task")),
        P(("rows", "task")),
        P(("rows", "task")),
        P("task", "rows"),
        P(),
    )
    out_specs = P("task", "rows")
    return jax.shard_map(local, mesh=mesh, in_specs=in_specs, out_specs=out_specs, check_vma=False)
```
